128 devices in a mesh: row: 16 (over z_hi, x, core), col: 8 (over y, z_lo).
Axes of the slice: x: 4, y: 4, z: 4 (z_hi: 2, z_lo: 2; z = z_hi * 2 + z_lo), core: 2. Of those that a mesh axis runs over, the one named last changes fastest.
Arguments:
- pair: bfloat16 [512, 512, 128], P('row', 'col'), may hold values from -6 to 6
- residue_mask: int32 [512], replicated, may hold values 0 or 1
- in_gain: float32 [2, 128], replicated, may hold values from 0.1 to 1.9
- proj_weight: bfloat16 [2, 128, 512], replicated, may hold values from -0.5 to 0.5
- gate_weight: bfloat16 [2, 128, 128], replicated, may hold values from -0.5 to 0.5
- out_gain: float32 [2, 128], replicated, may hold values from 0.1 to 1.9
- out_weight: bfloat16 [2, 128, 128], replicated, may hold values from -0.5 to 0.5
Outputs:
- updated: bfloat16 [512, 512, 128], P('row', 'col')
The draws below stay inside these ranges and needn't reach their ends.
Inputs may be any that keep to these rules, and one draw needn't show every extreme that they name: `residue_mask`: 1 marks a present residue.
All inputs are finite; a program needn't handle non-finite values.
Results may differ from the reference program's by a relative error of at most 0.02.
Values may be sent and summed in bfloat16 or wider, within the bound.
A program may use at most 128 MiB of HBM per device.

```python
import jax
import jax.numpy as jnp
from jax import lax

C = 128
CH = 128
N = 512


def with_ends(drawn, key, smallest, largest):
    longest = drawn.shape.index(max(drawn.shape))
    spots = []
    for shift in (0, 1):
        where = [jax.random.randint(jax.random.fold_in(key, axis), (), 0, length) for axis, length in enumerate(drawn.shape)]
        where[longest] = (where[longest] + shift) % drawn.shape[longest]
        spots.append(tuple(where))
    return drawn.at[spots[0]].set(smallest).at[spots[1]].set(largest)


def block_scale(own_key, dims, pieces, least, high):
    gain = 1.0
    for axis_at, blocks in pieces:
        draws = jax.random.uniform(jax.random.fold_in(jax.random.fold_in(own_key, 6), axis_at), (blocks,), jnp.float32, least / len(pieces), high / len(pieces))
        gain = gain * jnp.repeat(jnp.exp(draws), dims[axis_at] // blocks).reshape((-1,) + (1,) * (len(dims) - 1 - axis_at))
    return gain


def normal_values(rng, dims, scale, limit, shards=(), held_as=jnp.bfloat16):
    result = scale * jax.random.normal(rng, dims, jnp.float32)
    if shards:
        result = result * block_scale(rng, dims, shards, -0.22, 0.18)
    return jnp.clip(result, -limit, limit).astype(held_as)


def setup_inputs(seed: int = 0) -> dict:
    streams_of = jax.random.split(jax.random.key(seed), 8)
    pair = normal_values(streams_of[0], (N, N, C), 1.0, 6.0, ((0, 16), (1, 8)))
    residue_mask = with_ends((jax.random.randint(streams_of[1], (N,), 0, 8) < 7).astype(jnp.int32), jax.random.fold_in(streams_of[1], 1), 0, 1)
    in_gain = jnp.clip(1.0 + 0.18 * jax.random.normal(streams_of[2], (2, C), jnp.float32), 0.1, 1.9)
    proj_weight = normal_values(streams_of[3], (2, C, 4 * CH), C ** -0.5, 0.5)
    gate_weight = normal_values(streams_of[4], (2, C, C), C ** -0.5, 0.5)
    out_gain = jnp.clip(1.0 + 0.18 * jax.random.normal(streams_of[5], (2, CH), jnp.float32), 0.1, 1.9)
    out_weight = normal_values(streams_of[6], (2, CH, C), CH ** -0.5, 0.5)
    return {"pair": pair, "residue_mask": residue_mask, "in_gain": in_gain, "proj_weight": proj_weight, "gate_weight": gate_weight, "out_gain": out_gain, "out_weight": out_weight}


def layer_norm(values, scale_gain):
    values = values.astype(jnp.float32)
    center = lax.optimization_barrier(jnp.mean(values, axis=-1, keepdims=True))
    spread = lax.optimization_barrier(jnp.mean(jnp.square(values - center), axis=-1, keepdims=True))
    return (values - center) / jnp.sqrt(spread + 1e-05) * scale_gain.astype(jnp.float32)

def reference(pair, residue_mask, in_gain, proj_weight, gate_weight, out_gain, out_weight):
    flags = residue_mask.astype(jnp.float32)
    pair_weight = (flags[:, None] * flags[None, :])[:, :, None]
    state = pair
    hidden = proj_weight.shape[2] // 4
    for section in range(2):
        normed = layer_norm(state, in_gain[section]).astype(jnp.bfloat16)
        projected = jnp.dot(normed, proj_weight[section], preferred_element_type=jnp.float32)
        left_proj = (jax.nn.sigmoid(projected[..., :hidden]) * projected[..., hidden:2 * hidden] * pair_weight).astype(jnp.bfloat16)
        right_proj = (jax.nn.sigmoid(projected[..., 2 * hidden:3 * hidden]) * projected[..., 3 * hidden:] * pair_weight).astype(jnp.bfloat16)
        gate_value = jax.nn.sigmoid(jnp.dot(normed, gate_weight[section], preferred_element_type=jnp.float32)).astype(jnp.bfloat16)
        left_wide = jnp.transpose(left_proj.astype(jnp.float32), (2, 0, 1))
        right_wide = jnp.transpose(right_proj.astype(jnp.float32), (2, 0, 1))
        if section == 0:
            summed = jnp.einsum('cik,cjk->cij', left_wide, right_wide)
        else:
            summed = jnp.einsum('cki,ckj->cij', left_wide, right_wide)
        product = jnp.transpose(summed, (1, 2, 0))
        normout = layer_norm(product, out_gain[section]).astype(jnp.bfloat16)
        update = jnp.dot(normout, out_weight[section], preferred_element_type=jnp.float32)
        state = (state.astype(jnp.float32) + gate_value.astype(jnp.float32) * update).astype(jnp.bfloat16)
    return state
```

```python
import jax
import jax.numpy as jnp
from jax import lax
from jax.experimental import pallas as pl
from jax.experimental.pallas import tpu as pltpu
from jax.sharding import PartitionSpec as P

EPSILON = 1e-05
MESH = pl.DeviceIdType.MESH
DEVICES = 128
C = 128
ROWS = 32
COLS = 64
HALF = ROWS // 2
TILES = 16


def coords():
    r = lax.axis_index("row")
    c = lax.axis_index("col")
    return lax.rem(r // 2, 4), c // 2, (r // 8) * 2 + lax.rem(c, 2), lax.rem(r, 2)


def device_at(x, y, z, k):
    return ((z // 2) * 8 + x * 2 + k, y * 2 + lax.rem(z, 2))


def wrap(a):
    return lax.rem(a + 4, 4)


def enter(stage_sem):
    x, y, z, k = coords()
    xs = [device_at(wrap(x + a), y, z, k) for a in (1, 2, 3)]
    ys = [device_at(x, wrap(y + a), z, k) for a in (1, 2, 3)]
    zs = [device_at(x, y, wrap(z + a), k) for a in (1, 2, 3)]
    ks = [device_at(x, y, z, 1 - k)]
    barrier = pltpu.get_barrier_semaphore()
    for peer in xs + ys + zs + ks:
        pl.semaphore_signal(barrier, inc=1, device_id=peer, device_id_type=MESH)
    pl.semaphore_wait(barrier, 10)
    for stage, peers in enumerate((ys, zs, ks)):
        for peer in peers:
            pl.semaphore_signal(stage_sem.at[stage], inc=1, device_id=peer, device_id_type=MESH)
        pl.semaphore_wait(stage_sem.at[stage], len(peers))


def exchange(send, recv, send_sem, recv_sem):
    x, y, z, k = coords()
    me = lax.axis_index("row") * 8 + lax.axis_index("col")

    def step(s, carry):
        dx, dy, dz, dk = lax.rem(s, 4), lax.rem(s // 4, 4), lax.rem(s // 16, 4), s // 64
        row, col = device_at(wrap(x + dx), wrap(y + dy), wrap(z + dz), lax.rem(k + dk, 2))
        pltpu.make_async_remote_copy(
            send.at[row * 8 + col],
            recv.at[me],
            send_sem,
            recv_sem,
            device_id=(row, col),
            device_id_type=MESH,
        ).start()
        return carry

    lax.fori_loop(1, DEVICES, step, 0)
    recv[me] = send[me]


def wait_bytes(buffer, sem):
    part = buffer.at[pl.ds(0, DEVICES - 1)]
    pltpu.make_async_copy(part, part, sem).wait()


def normalise(values, gain):
    center = jnp.mean(values, axis=0, keepdims=True)
    moved = values - center
    spread = jnp.mean(moved * moved, axis=0, keepdims=True)
    return moved * lax.rsqrt(spread + EPSILON) * gain


def kernel(
    mask_ref,
    pair_ref,
    in_gain_ref,
    proj_ref,
    gate_ref,
    out_gain_ref,
    outw_ref,
    out_ref,
    proj_t,
    outw_t,
    in_gain_t,
    out_gain_t,
    weight_of,
    state,
    gate,
    left_f,
    right_f,
    sides_s,
    sides_r,
    prod_s,
    prod_r,
    left_m,
    right_m,
    stage_sem,
    send_sem,
    recv_sem,
):
    row_index = lax.axis_index("row")
    col_index = lax.axis_index("col")
    enter(stage_sem)

    lane = lax.broadcasted_iota(jnp.int32, (8, 128), 1)
    low = lane < COLS
    lane_col = lax.rem(lane, COLS)

    def add_col(j, flags):
        return jnp.where(lane_col == j, mask_ref[col_index * COLS + j].astype(jnp.float32), flags)

    col_flags = lax.fori_loop(0, COLS, add_col, jnp.zeros((8, 128), jnp.float32))
    for t in range(TILES):
        upper = mask_ref[row_index * ROWS + t].astype(jnp.float32)
        lower = mask_ref[row_index * ROWS + HALF + t].astype(jnp.float32)
        weight_of[t] = col_flags * jnp.where(low, upper, lower)

    for u in range(2):
        for n in range(4):
            block = proj_ref[u, :, n * 128 : (n + 1) * 128].astype(jnp.float32)
            proj_t[u, n * 128 : (n + 1) * 128, :] = block.T.astype(jnp.bfloat16)
        proj_t[u, 512:640, :] = gate_ref[u].astype(jnp.float32).T.astype(jnp.bfloat16)
        outw_t[u] = outw_ref[u].astype(jnp.float32).T.astype(jnp.bfloat16)
        in_gain_t[u] = jnp.broadcast_to(in_gain_ref[u : u + 1, :], (128, 128)).T
        out_gain_t[u] = jnp.broadcast_to(out_gain_ref[u : u + 1, :], (128, 128)).T

    def project(u, t, values):
        normed = normalise(values, in_gain_t[u]).astype(jnp.bfloat16)
        projected = jnp.dot(proj_t[u], normed, preferred_element_type=jnp.float32)
        weight = weight_of[t][0:1, :]
        left = jax.nn.sigmoid(projected[0:128]) * projected[128:256] * weight
        right = jax.nn.sigmoid(projected[256:384]) * projected[384:512] * weight
        left_f[pl.ds(t, C, stride=TILES), :] = left
        right_f[pl.ds(t, C, stride=TILES), :] = right
        gate[t] = jax.nn.sigmoid(projected[512:640])

    def pack(u):
        def step(c, carry):
            at = pl.ds(pl.multiple_of(c * TILES, TILES), TILES)
            sides_s[u, c, 0:16, :] = left_f[at, :].astype(jnp.bfloat16)
            sides_s[u, c, 16:32, :] = right_f[at, :].astype(jnp.bfloat16)
            return carry

        lax.fori_loop(0, C, step, 0)

    def first(t, carry):
        block = jnp.concatenate([pair_ref[t], pair_ref[t + HALF]], axis=0).astype(jnp.float32).T
        state[t] = block
        project(0, t, block)
        return carry

    lax.fori_loop(0, TILES, first, 0)

    low16 = lax.broadcasted_iota(jnp.int32, (16, 128), 1) < COLS

    def swap(a, b):
        a = a.astype(jnp.float32)
        b = b.astype(jnp.float32)
        one = jnp.where(low16, a, pltpu.roll(b, COLS, 1))
        two = jnp.where(low16, pltpu.roll(a, COLS, 1), b)
        return one.astype(jnp.bfloat16), two.astype(jnp.bfloat16)

    for u in range(2):
        pack(u)
        exchange(sides_s.at[u], sides_r.at[u], send_sem.at[2 * u], recv_sem.at[2 * u])
        wait_bytes(sides_r.at[u], recv_sem.at[2 * u])

        def assemble(r, carry):
            at = pl.multiple_of(r * ROWS, ROWS)
            for m in range(4):
                for side, whole in ((0, left_m), (16, right_m)):
                    one, two = swap(
                        sides_r[u, r * 8 + 2 * m, side : side + 16, :],
                        sides_r[u, r * 8 + 2 * m + 1, side : side + 16, :],
                    )
                    whole[pl.ds(at, 16), m * 128 : (m + 1) * 128] = one
                    whole[pl.ds(at + 16, 16), m * 128 : (m + 1) * 128] = two
            return carry

        lax.fori_loop(0, 16, assemble, 0)
        for q in range(4):
            if u == 0:
                dims = (((1,), (1,)), ((), ()))
                part = left_m[q * 128 : (q + 1) * 128, :]
            else:
                dims = (((0,), (0,)), ((), ()))
                part = left_m[:, q * 128 : (q + 1) * 128]
            product = lax.dot_general(part, right_m[...], dims, preferred_element_type=jnp.float32)
            for r in range(4):
                for m in range(4):
                    one, two = swap(
                        product[r * 32 : r * 32 + 16, m * 128 : (m + 1) * 128],
                        product[r * 32 + 16 : r * 32 + 32, m * 128 : (m + 1) * 128],
                    )
                    prod_s[u, (q * 4 + r) * 8 + 2 * m] = one
                    prod_s[u, (q * 4 + r) * 8 + 2 * m + 1] = two
        exchange(prod_s.at[u], prod_r.at[u], send_sem.at[2 * u + 1], recv_sem.at[2 * u + 1])
        wait_bytes(prod_r.at[u], recv_sem.at[2 * u + 1])

        def unpack(c, carry):
            left_f[pl.ds(pl.multiple_of(c * TILES, TILES), TILES), :] = prod_r[u, c].astype(jnp.float32)
            return carry

        lax.fori_loop(0, C, unpack, 0)

        def finish(t, carry):
            product = left_f[pl.ds(t, C, stride=TILES), :]
            normout = normalise(product, out_gain_t[u]).astype(jnp.bfloat16)
            update = jnp.dot(outw_t[u], normout, preferred_element_type=jnp.float32)
            new = (state[t] + gate[t] * update).astype(jnp.bfloat16).astype(jnp.float32)
            if u == 0:
                state[t] = new
            else:
                back = new.T.astype(jnp.bfloat16)
                out_ref[t] = back[0:COLS]
                out_ref[t + HALF] = back[COLS : 2 * COLS]
            return carry

        lax.fori_loop(0, TILES, finish, 0)
        if u == 0:

            def second(t, carry):
                project(1, t, state[t])
                return carry

            lax.fori_loop(0, TILES, second, 0)

    for u in range(2):
        wait_bytes(sides_s.at[u], send_sem.at[2 * u])
        wait_bytes(prod_s.at[u], send_sem.at[2 * u + 1])


def shards(pair, residue_mask, in_gain, proj_weight, gate_weight, out_gain, out_weight):
    vmem = pl.BlockSpec(memory_space=pltpu.VMEM)
    return pl.pallas_call(
        kernel,
        out_shape=jax.ShapeDtypeStruct(pair.shape, pair.dtype),
        in_specs=[pl.BlockSpec(memory_space=pltpu.SMEM)] + [vmem] * 6,
        out_specs=vmem,
        scratch_shapes=[
            pltpu.VMEM((2, 640, 128), jnp.bfloat16),
            pltpu.VMEM((2, 128, 128), jnp.bfloat16),
            pltpu.VMEM((2, 128, 128), jnp.float32),
            pltpu.VMEM((2, 128, 128), jnp.float32),
            pltpu.VMEM((TILES, 8, 128), jnp.float32),
            pltpu.VMEM((TILES, 128, 128), jnp.float32),
            pltpu.VMEM((TILES, 128, 128), jnp.float32),
            pltpu.VMEM((C * TILES, 128), jnp.float32),
            pltpu.VMEM((C * TILES, 128), jnp.float32),
            pltpu.VMEM((2, DEVICES, 32, 128), jnp.bfloat16),
            pltpu.VMEM((2, DEVICES, 32, 128), jnp.bfloat16),
            pltpu.VMEM((2, DEVICES, 16, 128), jnp.bfloat16),
            pltpu.VMEM((2, DEVICES, 16, 128), jnp.bfloat16),
            pltpu.VMEM((512, 512), jnp.bfloat16),
            pltpu.VMEM((512, 512), jnp.bfloat16),
            pltpu.SemaphoreType.REGULAR((3,)),
            pltpu.SemaphoreType.DMA((4,)),
            pltpu.SemaphoreType.DMA((4,)),
        ],
        compiler_params=pltpu.CompilerParams(
            collective_id=0, has_side_effects=True, vmem_limit_bytes=48 * 1024 * 1024
        ),
    )(residue_mask, pair, in_gain, proj_weight, gate_weight, out_gain, out_weight)


def solution(mesh):
    placed = (P("row", "col", None), P(), P(), P(), P(), P(), P())
    return jax.shard_map(
        shards, mesh=mesh, in_specs=placed, out_specs=P("row", "col", None), check_vma=False
    )
```

```python
import jax
import jax.numpy as jnp
from jax import lax
from jax.experimental import pallas as pl
from jax.experimental.pallas import tpu as pltpu
from jax.sharding import PartitionSpec as P

EPSILON = 1e-05
MESH = pl.DeviceIdType.MESH
DEVICES = 128
C = 128
ROWS = 32
COLS = 64
HALF = ROWS // 2
TILES = 16
PAIRS = 8
PARTS = 2


def coords():
    r = lax.axis_index("row")
    c = lax.axis_index("col")
    return lax.rem(r // 2, 4), c // 2, (r // 8) * 2 + lax.rem(c, 2), lax.rem(r, 2)


def device_at(x, y, z, k):
    return ((z // 2) * 8 + x * 2 + k, y * 2 + lax.rem(z, 2))


def wrap(a):
    return lax.rem(a + 4, 4)


def far_first(q):
    return jnp.where(q == 0, 2, jnp.where(q == 3, 0, q * 2 - 1))


def peer_at(s):
    x, y, z, _ = coords()
    a, b, c = lax.rem(s, 4), lax.rem(s // 4, 4), s // 16
    dx = far_first(a)
    dy = far_first(lax.rem(a + b, 4))
    dz = far_first(lax.rem(a + b + c, 4))
    return wrap(x + dx), wrap(y + dy), wrap(z + dz)


def greet():
    barrier = pltpu.get_barrier_semaphore()
    me = lax.axis_index("row") * 8 + lax.axis_index("col")

    def step(s, carry):
        peer = lax.rem(me + s, DEVICES)
        pl.semaphore_signal(
            barrier, inc=1, device_id=(peer // 8, lax.rem(peer, 8)), device_id_type=MESH
        )
        return carry

    lax.fori_loop(1, DEVICES, step, 0)


def send_all(send, recv, send_sem, recv_sem, core):
    _, _, _, k = coords()
    me = lax.axis_index("row") * 8 + lax.axis_index("col")

    def one(s):
        row, col = device_at(*peer_at(s), core)
        pltpu.make_async_remote_copy(
            send.at[row * 8 + col],
            recv.at[me],
            send_sem,
            recv_sem,
            device_id=(row, col),
            device_id_type=MESH,
        ).start()

    def step(s, carry):
        one(s)
        return carry

    lax.fori_loop(0, HERE, step, 0)
    lax.fori_loop(HERE + 1, 64, step, 0)

    @pl.when(k == core)
    def _():
        pltpu.make_async_copy(send.at[me], recv.at[me], recv_sem).start()

    @pl.when(k != core)
    def _():
        one(HERE)


def number_here():
    for s in range(64):
        a, b, c = s % 4, s // 4 % 4, s // 16
        order = (2, 1, 3, 0)
        if order[a] == order[(a + b) % 4] == order[(a + b + c) % 4] == 0:
            return s


HERE = number_here()


def wait_bytes(buffer, sem, count):
    part = buffer.at[pl.ds(0, count)]
    pltpu.make_async_copy(part, part, sem).wait()


def sigmoid(v):
    return 0.5 * jnp.tanh(0.5 * v) + 0.5


def normalise(values, gain):
    center = jnp.mean(values, axis=0, keepdims=True)
    moved = values - center
    spread = jnp.mean(moved * moved, axis=0, keepdims=True)
    return moved * lax.rsqrt(spread + EPSILON) * gain


def kernel(
    mask_hbm,
    pair_hbm,
    in_gain_hbm,
    proj_hbm,
    gate_hbm,
    out_gain_hbm,
    outw_hbm,
    out_ref,
    mask_ref,
    pair_ref,
    in_gain_ref,
    proj_ref,
    gate_ref,
    out_gain_ref,
    outw_ref,
    proj_t,
    outw_t,
    in_gain_t,
    out_gain_t,
    weight_of,
    state,
    gate,
    left_f,
    right_f,
    sides_s,
    sides_r,
    prod_s,
    prod_r,
    left_m,
    right_m,
    in_sem,
    send_sem,
    recv_sem,
):
    row_index = lax.axis_index("row")
    col_index = lax.axis_index("col")
    _, _, _, core = coords()
    loads = [
        pltpu.make_async_copy(source, target, in_sem.at[n])
        for n, (source, target) in enumerate(
            (
                (mask_hbm, mask_ref),
                (proj_hbm, proj_ref),
                (gate_hbm, gate_ref),
                (in_gain_hbm, in_gain_ref),
                (pair_hbm, pair_ref),
                (out_gain_hbm, out_gain_ref),
                (outw_hbm, outw_ref),
            )
        )
    ]
    for load in loads:
        load.start()
    greet()

    def turn(u):
        for n in range(4):
            block = proj_ref[u, :, n * 128 : (n + 1) * 128].astype(jnp.float32)
            proj_t[u, n * 128 : (n + 1) * 128, :] = block.T.astype(jnp.bfloat16)
        proj_t[u, 512:640, :] = gate_ref[u].astype(jnp.float32).T.astype(jnp.bfloat16)
        in_gain_t[u] = jnp.broadcast_to(in_gain_ref[u : u + 1, :], (128, 128)).T

    def turn_out(u):
        outw_t[u] = outw_ref[u].astype(jnp.float32).T.astype(jnp.bfloat16)
        out_gain_t[u] = jnp.broadcast_to(out_gain_ref[u : u + 1, :], (128, 128)).T

    loads[0].wait()
    lane = lax.broadcasted_iota(jnp.int32, (8, 128), 1)
    low = lane < COLS
    lane_col = lax.rem(lane, COLS)
    col_flags = jnp.zeros((8, 128), jnp.float32)
    for j in range(COLS):
        flag = mask_ref[col_index * COLS + j].astype(jnp.float32)
        col_flags = jnp.where(lane_col == j, flag, col_flags)
    for t in range(TILES):
        upper = mask_ref[row_index * ROWS + t].astype(jnp.float32)
        lower = mask_ref[row_index * ROWS + HALF + t].astype(jnp.float32)
        weight_of[t // 2, :, t % 2 * 128 : t % 2 * 128 + 128] = col_flags * jnp.where(low, upper, lower)
    for n in (1, 2, 3):
        loads[n].wait()
    turn(0)
    loads[4].wait()

    def wide(column):
        return jnp.concatenate([column, column], axis=1)

    def project(u, p, values):
        normed = normalise(values, wide(in_gain_t[u])).astype(jnp.bfloat16)
        weight = weight_of[p][0:1, :]

        def times(n):
            return jnp.dot(
                proj_t[u, n * 128 : (n + 1) * 128, :], normed, preferred_element_type=jnp.float32
            )

        left = sigmoid(times(0)) * (times(1) * weight)
        right = sigmoid(times(2)) * (times(3) * weight)
        for j in range(2):
            left_f[pl.ds(p * 2 + j, C, stride=TILES), :] = left[:, j * 128 : j * 128 + 128]
            right_f[pl.ds(p * 2 + j, C, stride=TILES), :] = right[:, j * 128 : j * 128 + 128]
        gate[p] = sigmoid(times(4))

    def pack(u, part):
        def step(c, carry):
            at = pl.ds(pl.multiple_of(c * TILES + part * 8, 8), 8)
            both = jnp.concatenate([left_f[at, :], right_f[at, :]], axis=0)
            sides_s[u, part, c] = both.astype(jnp.bfloat16)
            return carry

        lax.fori_loop(0, C, step, 0, unroll=8)

    def send_sides(u, part, k):
        send_all(
            sides_s.at[u, part], sides_r.at[u, part], send_sem.at[u], recv_sem.at[u], k
        )

    def send_products(u):
        for k in range(2):
            send_all(
                prod_s.at[u], prod_r.at[u], send_sem.at[2 + u], recv_sem.at[2 + u], k
            )

    def first(p, carry):
        tiles = [
            jnp.concatenate([pair_ref[p * 2 + j], pair_ref[p * 2 + j + HALF]], axis=0)
            .astype(jnp.float32)
            .T
            for j in range(2)
        ]
        block = jnp.concatenate(tiles, axis=1)
        state[p] = block
        project(0, p, block)
        return carry

    lax.fori_loop(0, PAIRS // 2, first, 0, unroll=2)
    pack(0, 0)
    pl.semaphore_wait(pltpu.get_barrier_semaphore(), DEVICES - 1)
    send_sides(0, 0, 0)
    send_sides(0, 0, 1)
    lax.fori_loop(PAIRS // 2, PAIRS, first, 0, unroll=2)
    pack(0, 1)
    send_sides(0, 1, 0)
    send_sides(0, 1, 1)
    for n in (5, 6):
        loads[n].wait()
    turn_out(0)
    turn(1)
    turn_out(1)

    def swap(a, b):
        one = jnp.where(low, a, pltpu.roll(b, COLS, 1))
        two = jnp.where(low, pltpu.roll(a, COLS, 1), b)
        return one, two

    for u in range(2):
        whole = sides_r.at[u]
        pltpu.make_async_copy(whole, whole, recv_sem.at[u]).wait()

        def assemble(r, carry):
            at = pl.multiple_of(r * ROWS, ROWS)
            for m in range(4):
                tiles = [
                    [sides_r[u, part, r * 8 + 2 * m + j].astype(jnp.float32) for part in range(2)]
                    for j in range(2)
                ]
                for side, target in ((0, left_m), (8, right_m)):
                    turned = [
                        swap(tiles[0][part][side : side + 8], tiles[1][part][side : side + 8])
                        for part in range(2)
                    ]
                    for h in range(2):
                        both = jnp.concatenate([turned[0][h], turned[1][h]], axis=0)
                        target[pl.ds(at + 16 * h, 16), m * 128 : (m + 1) * 128] = both.astype(
                            jnp.bfloat16
                        )
            return carry

        lax.fori_loop(0, 16, assemble, 0, unroll=2)
        for q in range(4):
            if u == 0:
                dims = (((1,), (1,)), ((), ()))
                part = left_m[q * 128 : (q + 1) * 128, :]
            else:
                dims = (((0,), (0,)), ((), ()))
                part = left_m[:, q * 128 : (q + 1) * 128]
            product = lax.dot_general(part, right_m[...], dims, preferred_element_type=jnp.float32)
            for r in range(4):
                for m in range(4):
                    turned = [
                        swap(
                            product[r * 32 + e : r * 32 + e + 8, m * 128 : (m + 1) * 128],
                            product[r * 32 + 16 + e : r * 32 + 24 + e, m * 128 : (m + 1) * 128],
                        )
                        for e in (0, 8)
                    ]
                    for h in range(2):
                        both = jnp.concatenate([turned[0][h], turned[1][h]], axis=0)
                        prod_s[u, (q * 4 + r) * 8 + 2 * m + h] = both.astype(jnp.bfloat16)
        send_products(u)
        whole = prod_r.at[u]
        pltpu.make_async_copy(whole, whole, recv_sem.at[2 + u]).wait()

        def unpack(c, carry):
            left_f[pl.ds(pl.multiple_of(c * TILES, TILES), TILES), :] = prod_r[u, c].astype(jnp.float32)
            return carry

        lax.fori_loop(0, C, unpack, 0, unroll=8)

        def finish(p, carry):
            product = jnp.concatenate(
                [left_f[pl.ds(p * 2 + j, C, stride=TILES), :] for j in range(2)], axis=1
            )
            normout = normalise(product, wide(out_gain_t[u])).astype(jnp.bfloat16)
            update = jnp.dot(outw_t[u], normout, preferred_element_type=jnp.float32)
            new = (state[p] + gate[p] * update).astype(jnp.bfloat16).astype(jnp.float32)
            if u == 0:
                state[p] = new
            else:
                for j in range(2):
                    back = new[:, j * 128 : j * 128 + 128].T.astype(jnp.bfloat16)
                    out_ref[p * 2 + j] = back[0:COLS]
                    out_ref[p * 2 + j + HALF] = back[COLS : 2 * COLS]
            return carry

        if u == 0:

            def second(p, carry):
                project(1, p, state[p])
                return carry

            lax.fori_loop(0, PAIRS, finish, 0, unroll=4)
            for part in range(PARTS):
                lax.fori_loop(part * 4, part * 4 + 4, second, 0, unroll=2)
                pack(1, part)
                send_sides(1, part, 0)
                send_sides(1, part, 1)
        else:
            lax.fori_loop(0, PAIRS, finish, 0, unroll=4)

    for u in range(2):
        for part in range(PARTS):
            wait_bytes(sides_s.at[u, part], send_sem.at[u], DEVICES - 1)
        wait_bytes(prod_s.at[u], send_sem.at[2 + u], DEVICES - 1)


def shards(pair, residue_mask, in_gain, proj_weight, gate_weight, out_gain, out_weight):
    return pl.pallas_call(
        kernel,
        out_shape=jax.ShapeDtypeStruct(pair.shape, pair.dtype),
        in_specs=[pl.BlockSpec(memory_space=pl.ANY)] * 7,
        out_specs=pl.BlockSpec(memory_space=pltpu.VMEM),
        scratch_shapes=[
            pltpu.SMEM(residue_mask.shape, residue_mask.dtype),
            pltpu.VMEM(pair.shape, pair.dtype),
            pltpu.VMEM(in_gain.shape, in_gain.dtype),
            pltpu.VMEM(proj_weight.shape, proj_weight.dtype),
            pltpu.VMEM(gate_weight.shape, gate_weight.dtype),
            pltpu.VMEM(out_gain.shape, out_gain.dtype),
            pltpu.VMEM(out_weight.shape, out_weight.dtype),
            pltpu.VMEM((2, 640, 128), jnp.bfloat16),
            pltpu.VMEM((2, 128, 128), jnp.bfloat16),
            pltpu.VMEM((2, 128, 128), jnp.float32),
            pltpu.VMEM((2, 128, 128), jnp.float32),
            pltpu.VMEM((PAIRS, 8, 256), jnp.float32),
            pltpu.VMEM((PAIRS, 128, 256), jnp.float32),
            pltpu.VMEM((PAIRS, 128, 256), jnp.float32),
            pltpu.VMEM((C * TILES, 128), jnp.float32),
            pltpu.VMEM((C * TILES, 128), jnp.float32),
            pltpu.VMEM((2, PARTS, DEVICES, 16, 128), jnp.bfloat16),
            pltpu.VMEM((2, PARTS, DEVICES, 16, 128), jnp.bfloat16),
            pltpu.VMEM((2, DEVICES, 16, 128), jnp.bfloat16),
            pltpu.VMEM((2, DEVICES, 16, 128), jnp.bfloat16),
            pltpu.VMEM((512, 512), jnp.bfloat16),
            pltpu.VMEM((512, 512), jnp.bfloat16),
            pltpu.SemaphoreType.DMA((7,)),
            pltpu.SemaphoreType.DMA((4,)),
            pltpu.SemaphoreType.DMA((4,)),
        ],
        compiler_params=pltpu.CompilerParams(
            collective_id=0, has_side_effects=True, vmem_limit_bytes=48 * 1024 * 1024
        ),
    )(residue_mask, pair, in_gain, proj_weight, gate_weight, out_gain, out_weight)


def solution(mesh):
    placed = (P("row", "col", None), P(), P(), P(), P(), P(), P())
    return jax.shard_map(
        shards, mesh=mesh, in_specs=placed, out_specs=P("row", "col", None), check_vma=False
    )
```

```python
import functools

import jax
import jax.numpy as jnp
from jax import lax
from jax.experimental import pallas as pl
from jax.experimental.pallas import tpu as pltpu
from jax.sharding import PartitionSpec as P

EPSILON = 1e-05
MESH = pl.DeviceIdType.MESH
DEVICES = 128
C = 128
ROWS = 32
COLS = 64
HALF = ROWS // 2
TILES = 16
PAIRS = 8
PARTS = 2


def coords():
    r = lax.axis_index("row")
    c = lax.axis_index("col")
    return lax.rem(r // 2, 4), c // 2, (r // 8) * 2 + lax.rem(c, 2), lax.rem(r, 2)


def device_at(x, y, z, k):
    return ((z // 2) * 8 + x * 2 + k, y * 2 + lax.rem(z, 2))


def wrap(a):
    return lax.rem(a + 4, 4)


def offsets():
    far = (2, 1, 3, 0)
    found = []
    for s in range(DEVICES):
        a, b, c, d = s % 4, s // 4 % 4, s // 16 % 4, 1 - s // 64
        found.append((far[a], far[(a + b) % 4], far[(a + b + c) % 4], d))
    found.remove((0, 0, 0, 0))
    return found


def peers():
    x, y, z, k = coords()
    rows = [[wrap(x + a) * 2 + (k if d == 0 else 1 - k) for a in range(4)] for d in range(2)]
    cols = [wrap(y + a) * 2 for a in range(4)]
    highs = [wrap(z + a) // 2 * 8 for a in range(4)]
    lows = [lax.rem(wrap(z + a), 2) for a in range(4)]
    return [(highs[c] + rows[d][a], cols[b] + lows[c]) for a, b, c, d in offsets()]


def greet():
    barrier = pltpu.get_barrier_semaphore()
    me = lax.axis_index("row") * 8 + lax.axis_index("col")

    def step(s, carry):
        peer = lax.rem(me + s, DEVICES)
        pl.semaphore_signal(
            barrier, inc=1, device_id=(peer // 8, lax.rem(peer, 8)), device_id_type=MESH
        )
        return carry

    lax.fori_loop(1, DEVICES, step, 0)


def send_all(others, send, recv, send_sem, recv_sem):
    me = lax.axis_index("row") * 8 + lax.axis_index("col")
    for row, col in others:
        pltpu.make_async_remote_copy(
            send.at[row * 8 + col],
            recv.at[me],
            send_sem,
            recv_sem,
            device_id=(row, col),
            device_id_type=MESH,
        ).start()
    recv[me] = send[me]


def wait_bytes(buffer, sem, count):
    part = buffer.at[pl.ds(0, count)]
    pltpu.make_async_copy(part, part, sem).wait()


def sigmoid(v):
    return 0.5 * jnp.tanh(0.5 * v) + 0.5


def normalise(values, gain):
    center = jnp.mean(values, axis=0, keepdims=True)
    moved = values - center
    spread = jnp.mean(moved * moved, axis=0, keepdims=True)
    return moved * lax.rsqrt(spread + EPSILON) * gain


def kernel(
    mask_hbm,
    pair_hbm,
    in_gain_hbm,
    proj_hbm,
    gate_hbm,
    out_gain_hbm,
    outw_hbm,
    out_hbm,
    out_ref,
    mask_ref,
    pair_ref,
    in_gain_ref,
    proj_ref,
    gate_ref,
    out_gain_ref,
    outw_ref,
    proj_t,
    outw_t,
    in_gain_t,
    out_gain_t,
    weight_of,
    state,
    gate,
    left_f,
    right_f,
    sides_s,
    sides_r,
    prod_s,
    prod_r,
    prod_f,
    left_m,
    right_m,
    in_sem,
    out_sem,
    send_sem,
    recv_sem,
):
    row_index = lax.axis_index("row")
    col_index = lax.axis_index("col")
    others = peers()
    loads = [
        pltpu.make_async_copy(source, target, in_sem.at[n])
        for n, (source, target) in enumerate(
            (
                (mask_hbm, mask_ref),
                (proj_hbm, proj_ref),
                (gate_hbm, gate_ref),
                (in_gain_hbm, in_gain_ref),
                (pair_hbm, pair_ref),
                (out_gain_hbm, out_gain_ref),
                (outw_hbm, outw_ref),
            )
        )
    ]
    stores = [
        pltpu.make_async_copy(
            out_ref.at[pl.ds(part * 8 + h * HALF, 8)],
            out_hbm.at[pl.ds(part * 8 + h * HALF, 8)],
            out_sem.at[part * 2 + h],
        )
        for part in range(PARTS)
        for h in range(2)
    ]
    for load in loads:
        load.start()
    greet()

    def turn(u):
        for n in range(4):
            block = proj_ref[u, :, n * 128 : (n + 1) * 128].astype(jnp.float32)
            proj_t[u, n * 128 : (n + 1) * 128, :] = block.T.astype(jnp.bfloat16)
        proj_t[u, 512:640, :] = gate_ref[u].astype(jnp.float32).T.astype(jnp.bfloat16)
        in_gain_t[u] = jnp.broadcast_to(in_gain_ref[u : u + 1, :], (128, 128)).T

    def turn_out(u):
        outw_t[u] = outw_ref[u].astype(jnp.float32).T.astype(jnp.bfloat16)
        out_gain_t[u] = jnp.broadcast_to(out_gain_ref[u : u + 1, :], (128, 128)).T

    loads[0].wait()
    lane = lax.broadcasted_iota(jnp.int32, (8, 128), 1)
    low = lane < COLS
    lane_col = lax.rem(lane, COLS)
    col_flags = jnp.zeros((8, 128), jnp.float32)
    for j in range(COLS):
        flag = mask_ref[col_index * COLS + j].astype(jnp.float32)
        col_flags = jnp.where(lane_col == j, flag, col_flags)
    for t in range(TILES):
        upper = mask_ref[row_index * ROWS + t].astype(jnp.float32)
        lower = mask_ref[row_index * ROWS + HALF + t].astype(jnp.float32)
        weight_of[t // 2, :, t % 2 * 128 : t % 2 * 128 + 128] = col_flags * jnp.where(low, upper, lower)
    for n in (1, 2, 3):
        loads[n].wait()
    turn(0)
    loads[4].wait()

    def wide(column):
        return jnp.concatenate([column, column], axis=1)

    def project(u, p, values):
        normed = normalise(values, wide(in_gain_t[u])).astype(jnp.bfloat16)
        weight = weight_of[p][0:1, :]

        def times(n):
            return jnp.dot(
                proj_t[u, n * 128 : (n + 1) * 128, :], normed, preferred_element_type=jnp.float32
            )

        left = sigmoid(times(0)) * (times(1) * weight)
        right = sigmoid(times(2)) * (times(3) * weight)
        for j in range(2):
            left_f[pl.ds(p * 2 + j, C, stride=TILES), :] = left[:, j * 128 : j * 128 + 128]
            right_f[pl.ds(p * 2 + j, C, stride=TILES), :] = right[:, j * 128 : j * 128 + 128]
        gate[p] = sigmoid(times(4))

    def pack(u, part):
        def step(c, carry):
            at = pl.ds(pl.multiple_of(c * TILES + part * 8, 8), 8)
            both = jnp.concatenate([left_f[at, :], right_f[at, :]], axis=0)
            sides_s[u, part, c] = both.astype(jnp.bfloat16)
            return carry

        lax.fori_loop(0, C, step, 0, unroll=8)

    def send_sides(u, part):
        send_all(
            others,
            sides_s.at[u, part],
            sides_r.at[u, part],
            send_sem.at[2 * u + part],
            recv_sem.at[2 * u + part],
        )

    def first(p, carry):
        tiles = [
            jnp.concatenate([pair_ref[p * 2 + j], pair_ref[p * 2 + j + HALF]], axis=0)
            .astype(jnp.float32)
            .T
            for j in range(2)
        ]
        block = jnp.concatenate(tiles, axis=1)
        state[p] = block
        project(0, p, block)
        return carry

    lax.fori_loop(0, PAIRS // 2, first, 0, unroll=2)
    pack(0, 0)
    pl.semaphore_wait(pltpu.get_barrier_semaphore(), DEVICES - 1)
    send_sides(0, 0)
    lax.fori_loop(PAIRS // 2, PAIRS, first, 0, unroll=2)
    pack(0, 1)
    send_sides(0, 1)
    for n in (5, 6):
        loads[n].wait()
    turn_out(0)
    turn(1)
    turn_out(1)

    def swap(a, b):
        one = jnp.where(low, a, pltpu.roll(b, COLS, 1))
        two = jnp.where(low, pltpu.roll(a, COLS, 1), b)
        return one, two

    for u in range(2):

        def assemble(part, r, sides):
            for m in range(4):
                tiles = [
                    sides_r[u, part, r * 8 + 2 * m + j].astype(jnp.float32) for j in range(2)
                ]
                for side, target in sides:
                    both = jnp.concatenate(
                        swap(tiles[0][side : side + 8], tiles[1][side : side + 8]), axis=0
                    )
                    at = pl.multiple_of(part * 256 + r * 16, 16)
                    target[pl.ds(at, 16), m * 128 : (m + 1) * 128] = both.astype(jnp.bfloat16)

        def assemble_natural(r):
            for m in range(4):
                turned = []
                for part in range(PARTS):
                    tiles = [
                        sides_r[u, part, r * 8 + 2 * m + j].astype(jnp.float32) for j in range(2)
                    ]
                    turned.append(swap(tiles[0][8:16], tiles[1][8:16]))
                for h in range(2):
                    both = jnp.concatenate([turned[0][h], turned[1][h]], axis=0)
                    at = pl.multiple_of(r * ROWS + 16 * h, 16)
                    right_m[pl.ds(at, 16), m * 128 : (m + 1) * 128] = both.astype(jnp.bfloat16)

        def left_only(part, r):
            assemble(part, r, ((0, left_m),))

        def both_sides(part, r):
            assemble(part, r, ((0, left_m), (8, right_m)))

        def every(body):
            def step(r, carry):
                body(r)
                return carry

            lax.fori_loop(0, 16, step, 0, unroll=4)

        for part in range(PARTS):
            wait_bytes(sides_r.at[u, part], recv_sem.at[2 * u + part], DEVICES - 1)
            every(functools.partial(left_only if u == 0 else both_sides, part))
        if u == 0:
            every(assemble_natural)

        def deliver(upper, lower, r, m):
            turned = [swap(upper[e], lower[e]) for e in range(2)]
            for h in range(2):
                both = jnp.concatenate([turned[0][h], turned[1][h]], axis=0)
                prod_s[u, r * 8 + 2 * m + h] = both.astype(jnp.bfloat16)

        for q in range(4):
            if u == 0:
                rows = jnp.concatenate(
                    [left_m[part * 256 + q * 64 : part * 256 + q * 64 + 64, :] for part in range(2)],
                    axis=0,
                )
                product = lax.dot_general(
                    rows,
                    right_m[...],
                    (((1,), (1,)), ((), ())),
                    preferred_element_type=jnp.float32,
                )
            else:
                product = lax.dot_general(
                    left_m[:, q * 128 : (q + 1) * 128],
                    right_m[...],
                    (((0,), (0,)), ((), ())),
                    preferred_element_type=jnp.float32,
                )
            for r in range(4):
                for m in range(4):
                    across = slice(m * 128, (m + 1) * 128)
                    if u == 0:
                        starts = [[e * 64 + r * 16 + h * 8 for e in range(2)] for h in range(2)]
                    else:
                        starts = [[r * 32 + h * 16 + e * 8 for e in range(2)] for h in range(2)]
                    upper, lower = (
                        [product[at : at + 8, across] for at in starts[h]] for h in range(2)
                    )
                    deliver(upper, lower, q * 4 + r, m)
        send_all(others, prod_s.at[u], prod_r.at[u], send_sem.at[4 + u], recv_sem.at[4 + u])
        wait_bytes(prod_r.at[u], recv_sem.at[4 + u], DEVICES - 1)

        def unpack(c, carry):
            prod_f[pl.ds(pl.multiple_of(c * TILES, TILES), TILES), :] = prod_r[u, c].astype(jnp.float32)
            return carry

        lax.fori_loop(0, C, unpack, 0, unroll=8)

        def finish(p, carry):
            product = jnp.concatenate(
                [prod_f[pl.ds(p * 2 + j, C, stride=TILES), :] for j in range(2)], axis=1
            )
            normout = normalise(product, wide(out_gain_t[u])).astype(jnp.bfloat16)
            update = jnp.dot(outw_t[u], normout, preferred_element_type=jnp.float32)
            new = (state[p] + gate[p] * update).astype(jnp.bfloat16).astype(jnp.float32)
            if u == 0:
                state[p] = new
            else:
                for j in range(2):
                    back = new[:, j * 128 : j * 128 + 128].T.astype(jnp.bfloat16)
                    out_ref[p * 2 + j] = back[0:COLS]
                    out_ref[p * 2 + j + HALF] = back[COLS : 2 * COLS]
            return carry

        def second(p, carry):
            project(1, p, state[p])
            return carry

        for part in range(PARTS):
            lax.fori_loop(part * 4, part * 4 + 4, finish, 0, unroll=4)
            if u == 0:
                lax.fori_loop(part * 4, part * 4 + 4, second, 0, unroll=2)
                pack(1, part)
                send_sides(1, part)
            else:
                for h in range(2):
                    stores[part * 2 + h].start()

    for u in range(2):
        for part in range(PARTS):
            wait_bytes(sides_s.at[u, part], send_sem.at[2 * u + part], DEVICES - 1)
        wait_bytes(prod_s.at[u], send_sem.at[4 + u], DEVICES - 1)
    for store in stores:
        store.wait()


def shards(pair, residue_mask, in_gain, proj_weight, gate_weight, out_gain, out_weight):
    return pl.pallas_call(
        kernel,
        out_shape=jax.ShapeDtypeStruct(pair.shape, pair.dtype),
        in_specs=[pl.BlockSpec(memory_space=pl.ANY)] * 7,
        out_specs=pl.BlockSpec(memory_space=pl.ANY),
        scratch_shapes=[
            pltpu.VMEM(pair.shape, pair.dtype),
            pltpu.SMEM(residue_mask.shape, residue_mask.dtype),
            pltpu.VMEM(pair.shape, pair.dtype),
            pltpu.VMEM(in_gain.shape, in_gain.dtype),
            pltpu.VMEM(proj_weight.shape, proj_weight.dtype),
            pltpu.VMEM(gate_weight.shape, gate_weight.dtype),
            pltpu.VMEM(out_gain.shape, out_gain.dtype),
            pltpu.VMEM(out_weight.shape, out_weight.dtype),
            pltpu.VMEM((2, 640, 128), jnp.bfloat16),
            pltpu.VMEM((2, 128, 128), jnp.bfloat16),
            pltpu.VMEM((2, 128, 128), jnp.float32),
            pltpu.VMEM((2, 128, 128), jnp.float32),
            pltpu.VMEM((PAIRS, 8, 256), jnp.float32),
            pltpu.VMEM((PAIRS, 128, 256), jnp.float32),
            pltpu.VMEM((PAIRS, 128, 256), jnp.float32),
            pltpu.VMEM((C * TILES, 128), jnp.float32),
            pltpu.VMEM((C * TILES, 128), jnp.float32),
            pltpu.VMEM((2, PARTS, DEVICES, 16, 128), jnp.bfloat16),
            pltpu.VMEM((2, PARTS, DEVICES, 16, 128), jnp.bfloat16),
            pltpu.VMEM((2, DEVICES, 16, 128), jnp.bfloat16),
            pltpu.VMEM((2, DEVICES, 16, 128), jnp.bfloat16),
            pltpu.VMEM((C * TILES, 128), jnp.float32),
            pltpu.VMEM((512, 512), jnp.bfloat16),
            pltpu.VMEM((512, 512), jnp.bfloat16),
            pltpu.SemaphoreType.DMA((7,)),
            pltpu.SemaphoreType.DMA((4,)),
            pltpu.SemaphoreType.DMA((6,)),
            pltpu.SemaphoreType.DMA((6,)),
        ],
        compiler_params=pltpu.CompilerParams(
            collective_id=0, has_side_effects=True, vmem_limit_bytes=58 * 1024 * 1024
        ),
    )(residue_mask, pair, in_gain, proj_weight, gate_weight, out_gain, out_weight)


def solution(mesh):
    placed = (P("row", "col", None), P(), P(), P(), P(), P(), P())
    return jax.shard_map(
        shards, mesh=mesh, in_specs=placed, out_specs=P("row", "col", None), check_vma=False
    )
```

```python
import functools

import jax
import jax.numpy as jnp
from jax import lax
from jax.experimental import pallas as pl
from jax.experimental.pallas import tpu as pltpu
from jax.sharding import PartitionSpec as P

EPSILON = 1e-05
MESH = pl.DeviceIdType.MESH
DEVICES = 128
C = 128
ROWS = 32
COLS = 64
HALF = ROWS // 2
TILES = 16
PAIRS = 8
PARTS = 2


def coords():
    r = lax.axis_index("row")
    c = lax.axis_index("col")
    return lax.rem(r // 2, 4), c // 2, (r // 8) * 2 + lax.rem(c, 2), lax.rem(r, 2)


def device_at(x, y, z, k):
    return ((z // 2) * 8 + x * 2 + k, y * 2 + lax.rem(z, 2))


def wrap(a):
    return lax.rem(a + 4, 4)


def offsets():
    far = (2, 1, 3, 0)
    found = []
    for s in range(DEVICES):
        a, b, c, d = s % 4, s // 4 % 4, s // 16 % 4, 1 - s // 64
        found.append((far[a], far[(a + b) % 4], far[(a + b + c) % 4], d))
    found.remove((0, 0, 0, 0))
    return found


def peers():
    x, y, z, k = coords()
    rows = [[wrap(x + a) * 2 + (k if d == 0 else 1 - k) for a in range(4)] for d in range(2)]
    cols = [wrap(y + a) * 2 for a in range(4)]
    highs = [wrap(z + a) // 2 * 8 for a in range(4)]
    lows = [lax.rem(wrap(z + a), 2) for a in range(4)]
    return [(highs[c] + rows[d][a], cols[b] + lows[c]) for a, b, c, d in offsets()]


def greet(others):
    barrier = pltpu.get_barrier_semaphore()
    for peer in sorted_far(others):
        pl.semaphore_signal(barrier, inc=1, device_id=peer, device_id_type=MESH)


def sorted_far(others):
    far = [sum((0, 1, 2, 1)[v] for v in offset[:3]) for offset in offsets()]
    return [others[n] for n in sorted(range(DEVICES - 1), key=lambda n: -far[n])]


def send_all(others, send, recv, send_sem, recv_sem):
    me = lax.axis_index("row") * 8 + lax.axis_index("col")
    for row, col in others:
        pltpu.make_async_remote_copy(
            send.at[row * 8 + col],
            recv.at[me],
            send_sem,
            recv_sem,
            device_id=(row, col),
            device_id_type=MESH,
        ).start()
    recv[me] = send[me]


def wait_bytes(buffer, sem, count):
    part = buffer.at[pl.ds(0, count)]
    pltpu.make_async_copy(part, part, sem).wait()


def sigmoid(v):
    return 0.5 * jnp.tanh(0.5 * v) + 0.5


def normalise(values, gain):
    center = jnp.mean(values, axis=0, keepdims=True)
    moved = values - center
    spread = jnp.mean(moved * moved, axis=0, keepdims=True)
    return moved * lax.rsqrt(spread + EPSILON) * gain


def kernel(
    mask_hbm,
    pair_hbm,
    in_gain_hbm,
    proj_hbm,
    gate_hbm,
    out_gain_hbm,
    outw_hbm,
    out_hbm,
    out_ref,
    mask_ref,
    pair_ref,
    in_gain_ref,
    proj_ref,
    gate_ref,
    out_gain_ref,
    outw_ref,
    proj_t,
    outw_t,
    in_gain_t,
    out_gain_t,
    weight_of,
    state,
    gate,
    left_f,
    right_f,
    sides_s,
    sides_r,
    prod_s,
    prod_r,
    prod_f,
    left_m,
    right_m,
    in_sem,
    out_sem,
    send_sem,
    recv_sem,
):
    row_index = lax.axis_index("row")
    col_index = lax.axis_index("col")
    others = peers()
    loads = [
        pltpu.make_async_copy(source, target, in_sem.at[n])
        for n, (source, target) in enumerate(
            (
                (mask_hbm, mask_ref),
                (proj_hbm, proj_ref),
                (gate_hbm, gate_ref),
                (in_gain_hbm, in_gain_ref),
                (pair_hbm, pair_ref),
                (out_gain_hbm, out_gain_ref),
                (outw_hbm, outw_ref),
            )
        )
    ]
    stores = [
        pltpu.make_async_copy(
            out_ref.at[pl.ds(part * 8 + h * HALF, 8)],
            out_hbm.at[pl.ds(part * 8 + h * HALF, 8)],
            out_sem.at[part * 2 + h],
        )
        for part in range(PARTS)
        for h in range(2)
    ]
    for load in loads:
        load.start()
    greet(others)

    def turn(u):
        for n in range(4):
            block = proj_ref[u, :, n * 128 : (n + 1) * 128].astype(jnp.float32)
            proj_t[u, n * 128 : (n + 1) * 128, :] = block.T.astype(jnp.bfloat16)
        proj_t[u, 512:640, :] = gate_ref[u].astype(jnp.float32).T.astype(jnp.bfloat16)
        in_gain_t[u] = jnp.broadcast_to(in_gain_ref[u : u + 1, :], (128, 128)).T

    def turn_out(u):
        outw_t[u] = outw_ref[u].astype(jnp.float32).T.astype(jnp.bfloat16)
        out_gain_t[u] = jnp.broadcast_to(out_gain_ref[u : u + 1, :], (128, 128)).T

    loads[0].wait()
    lane = lax.broadcasted_iota(jnp.int32, (8, 128), 1)
    low = lane < COLS
    lane_col = lax.rem(lane, COLS)
    col_flags = jnp.zeros((8, 128), jnp.float32)
    for j in range(COLS):
        flag = mask_ref[col_index * COLS + j].astype(jnp.float32)
        col_flags = jnp.where(lane_col == j, flag, col_flags)
    for t in range(TILES):
        upper = mask_ref[row_index * ROWS + t].astype(jnp.float32)
        lower = mask_ref[row_index * ROWS + HALF + t].astype(jnp.float32)
        weight_of[t // 2, :, t % 2 * 128 : t % 2 * 128 + 128] = col_flags * jnp.where(low, upper, lower)
    for n in (1, 2, 3):
        loads[n].wait()
    turn(0)
    loads[4].wait()

    def wide(column):
        return jnp.concatenate([column, column], axis=1)

    def project(u, p, values):
        normed = normalise(values, wide(in_gain_t[u])).astype(jnp.bfloat16)
        weight = weight_of[p][0:1, :]

        def times(n):
            return jnp.dot(
                proj_t[u, n * 128 : (n + 1) * 128, :], normed, preferred_element_type=jnp.float32
            )

        left = sigmoid(times(0)) * (times(1) * weight)
        right = sigmoid(times(2)) * (times(3) * weight)
        for j in range(2):
            left_f[pl.ds(p * 2 + j, C, stride=TILES), :] = left[:, j * 128 : j * 128 + 128]
            right_f[pl.ds(p * 2 + j, C, stride=TILES), :] = right[:, j * 128 : j * 128 + 128]
        gate[p] = sigmoid(times(4))

    def pack(u, part):
        def step(c, carry):
            at = pl.ds(pl.multiple_of(c * TILES + part * 8, 8), 8)
            both = jnp.concatenate([left_f[at, :], right_f[at, :]], axis=0)
            sides_s[u, part, c] = both.astype(jnp.bfloat16)
            return carry

        lax.fori_loop(0, C, step, 0, unroll=8)

    def send_sides(u, part):
        send_all(
            others,
            sides_s.at[u, part],
            sides_r.at[u, part],
            send_sem.at[2 * u + part],
            recv_sem.at[2 * u + part],
        )

    def first(p, carry):
        tiles = [
            jnp.concatenate([pair_ref[p * 2 + j], pair_ref[p * 2 + j + HALF]], axis=0)
            .astype(jnp.float32)
            .T
            for j in range(2)
        ]
        block = jnp.concatenate(tiles, axis=1)
        state[p] = block
        project(0, p, block)
        return carry

    lax.fori_loop(0, PAIRS // 2, first, 0, unroll=2)
    pack(0, 0)
    pl.semaphore_wait(pltpu.get_barrier_semaphore(), DEVICES - 1)
    send_sides(0, 0)
    lax.fori_loop(PAIRS // 2, PAIRS, first, 0, unroll=2)
    pack(0, 1)
    send_sides(0, 1)
    for n in (5, 6):
        loads[n].wait()
    turn_out(0)
    turn(1)
    turn_out(1)

    def swap(a, b):
        one = jnp.where(low, a, pltpu.roll(b, COLS, 1))
        two = jnp.where(low, pltpu.roll(a, COLS, 1), b)
        return one, two

    for u in range(2):

        def assemble(part, r, sides):
            for m in range(4):
                tiles = [
                    sides_r[u, part, r * 8 + 2 * m + j].astype(jnp.float32) for j in range(2)
                ]
                for side, target in sides:
                    both = jnp.concatenate(
                        swap(tiles[0][side : side + 8], tiles[1][side : side + 8]), axis=0
                    )
                    at = pl.multiple_of(part * 256 + r * 16, 16)
                    target[pl.ds(at, 16), m * 128 : (m + 1) * 128] = both.astype(jnp.bfloat16)

        def assemble_natural(r):
            for m in range(4):
                turned = []
                for part in range(PARTS):
                    tiles = [
                        sides_r[u, part, r * 8 + 2 * m + j].astype(jnp.float32) for j in range(2)
                    ]
                    turned.append(swap(tiles[0][8:16], tiles[1][8:16]))
                for h in range(2):
                    both = jnp.concatenate([turned[0][h], turned[1][h]], axis=0)
                    at = pl.multiple_of(r * ROWS + 16 * h, 16)
                    right_m[pl.ds(at, 16), m * 128 : (m + 1) * 128] = both.astype(jnp.bfloat16)

        def left_only(part, r):
            assemble(part, r, ((0, left_m),))

        def both_sides(part, r):
            assemble(part, r, ((0, left_m), (8, right_m)))

        def every(body):
            def step(r, carry):
                body(r)
                return carry

            lax.fori_loop(0, 16, step, 0, unroll=4)

        for part in range(PARTS):
            wait_bytes(sides_r.at[u, part], recv_sem.at[2 * u + part], DEVICES - 1)
            every(functools.partial(left_only if u == 0 else both_sides, part))
        if u == 0:
            every(assemble_natural)

        def deliver(upper, lower, r, m):
            turned = [swap(upper[e], lower[e]) for e in range(2)]
            for h in range(2):
                both = jnp.concatenate([turned[0][h], turned[1][h]], axis=0)
                prod_s[u, r * 8 + 2 * m + h] = both.astype(jnp.bfloat16)

        for q in range(4):
            if u == 0:
                rows = jnp.concatenate(
                    [left_m[part * 256 + q * 64 : part * 256 + q * 64 + 64, :] for part in range(2)],
                    axis=0,
                )
                product = lax.dot_general(
                    rows,
                    right_m[...],
                    (((1,), (1,)), ((), ())),
                    preferred_element_type=jnp.float32,
                )
            else:
                product = lax.dot_general(
                    left_m[:, q * 128 : (q + 1) * 128],
                    right_m[...],
                    (((0,), (0,)), ((), ())),
                    preferred_element_type=jnp.float32,
                )
            for r in range(4):
                for m in range(4):
                    across = slice(m * 128, (m + 1) * 128)
                    if u == 0:
                        starts = [[e * 64 + r * 16 + h * 8 for e in range(2)] for h in range(2)]
                    else:
                        starts = [[r * 32 + h * 16 + e * 8 for e in range(2)] for h in range(2)]
                    upper, lower = (
                        [product[at : at + 8, across] for at in starts[h]] for h in range(2)
                    )
                    deliver(upper, lower, q * 4 + r, m)
        send_all(others, prod_s.at[u], prod_r.at[u], send_sem.at[4 + u], recv_sem.at[4 + u])
        wait_bytes(prod_r.at[u], recv_sem.at[4 + u], DEVICES - 1)

        def unpack(c, carry):
            prod_f[pl.ds(pl.multiple_of(c * TILES, TILES), TILES), :] = prod_r[u, c].astype(jnp.float32)
            return carry

        lax.fori_loop(0, C, unpack, 0, unroll=8)

        def finish(p, carry):
            product = jnp.concatenate(
                [prod_f[pl.ds(p * 2 + j, C, stride=TILES), :] for j in range(2)], axis=1
            )
            normout = normalise(product, wide(out_gain_t[u])).astype(jnp.bfloat16)
            update = jnp.dot(outw_t[u], normout, preferred_element_type=jnp.float32)
            new = (state[p] + gate[p] * update).astype(jnp.bfloat16).astype(jnp.float32)
            if u == 0:
                state[p] = new
            else:
                for j in range(2):
                    back = new[:, j * 128 : j * 128 + 128].T.astype(jnp.bfloat16)
                    out_ref[p * 2 + j] = back[0:COLS]
                    out_ref[p * 2 + j + HALF] = back[COLS : 2 * COLS]
            return carry

        def second(p, carry):
            project(1, p, state[p])
            return carry

        for part in range(PARTS):
            lax.fori_loop(part * 4, part * 4 + 4, finish, 0, unroll=4)
            if u == 0:
                lax.fori_loop(part * 4, part * 4 + 4, second, 0, unroll=2)
                pack(1, part)
                send_sides(1, part)
            else:
                for h in range(2):
                    stores[part * 2 + h].start()

    for u in range(2):
        for part in range(PARTS):
            wait_bytes(sides_s.at[u, part], send_sem.at[2 * u + part], DEVICES - 1)
        wait_bytes(prod_s.at[u], send_sem.at[4 + u], DEVICES - 1)
    for store in stores:
        store.wait()


def shards(pair, residue_mask, in_gain, proj_weight, gate_weight, out_gain, out_weight):
    return pl.pallas_call(
        kernel,
        out_shape=jax.ShapeDtypeStruct(pair.shape, pair.dtype),
        in_specs=[pl.BlockSpec(memory_space=pl.ANY)] * 7,
        out_specs=pl.BlockSpec(memory_space=pl.ANY),
        scratch_shapes=[
            pltpu.VMEM(pair.shape, pair.dtype),
            pltpu.SMEM(residue_mask.shape, residue_mask.dtype),
            pltpu.VMEM(pair.shape, pair.dtype),
            pltpu.VMEM(in_gain.shape, in_gain.dtype),
            pltpu.VMEM(proj_weight.shape, proj_weight.dtype),
            pltpu.VMEM(gate_weight.shape, gate_weight.dtype),
            pltpu.VMEM(out_gain.shape, out_gain.dtype),
            pltpu.VMEM(out_weight.shape, out_weight.dtype),
            pltpu.VMEM((2, 640, 128), jnp.bfloat16),
            pltpu.VMEM((2, 128, 128), jnp.bfloat16),
            pltpu.VMEM((2, 128, 128), jnp.float32),
            pltpu.VMEM((2, 128, 128), jnp.float32),
            pltpu.VMEM((PAIRS, 8, 256), jnp.float32),
            pltpu.VMEM((PAIRS, 128, 256), jnp.float32),
            pltpu.VMEM((PAIRS, 128, 256), jnp.float32),
            pltpu.VMEM((C * TILES, 128), jnp.float32),
            pltpu.VMEM((C * TILES, 128), jnp.float32),
            pltpu.VMEM((2, PARTS, DEVICES, 16, 128), jnp.bfloat16),
            pltpu.VMEM((2, PARTS, DEVICES, 16, 128), jnp.bfloat16),
            pltpu.VMEM((2, DEVICES, 16, 128), jnp.bfloat16),
            pltpu.VMEM((2, DEVICES, 16, 128), jnp.bfloat16),
            pltpu.VMEM((C * TILES, 128), jnp.float32),
            pltpu.VMEM((512, 512), jnp.bfloat16),
            pltpu.VMEM((512, 512), jnp.bfloat16),
            pltpu.SemaphoreType.DMA((7,)),
            pltpu.SemaphoreType.DMA((4,)),
            pltpu.SemaphoreType.DMA((6,)),
            pltpu.SemaphoreType.DMA((6,)),
        ],
        compiler_params=pltpu.CompilerParams(
            collective_id=0, has_side_effects=True, vmem_limit_bytes=58 * 1024 * 1024
        ),
    )(residue_mask, pair, in_gain, proj_weight, gate_weight, out_gain, out_weight)


def solution(mesh):
    placed = (P("row", "col", None), P(), P(), P(), P(), P(), P())
    return jax.shard_map(
        shards, mesh=mesh, in_specs=placed, out_specs=P("row", "col", None), check_vma=False
    )
```

```python
import jax
import jax.numpy as jnp
from jax import lax
from jax.experimental import pallas as pl
from jax.experimental.pallas import tpu as pltpu
from jax.sharding import PartitionSpec as P

EPSILON = 1e-05
MESH = pl.DeviceIdType.MESH
CHIPS = 64
C = 128
ROWS = 32
COLS = 64
HALF = ROWS // 2
TILES = 16
PAIRS = 8
PARTS = 2


def coords():
    r = lax.axis_index("row")
    c = lax.axis_index("col")
    return lax.rem(r // 2, 4), c // 2, (r // 8) * 2 + lax.rem(c, 2), lax.rem(r, 2)


def device_at(x, y, z, k):
    return ((z // 2) * 8 + x * 2 + k, y * 2 + lax.rem(z, 2))


def wrap(a):
    return lax.rem(a + 4, 4)


def offsets():
    far = (2, 1, 3, 0)
    found = []
    for s in range(CHIPS):
        a, b, c = s % 4, s // 4 % 4, s // 16
        found.append((far[a], far[(a + b) % 4], far[(a + b + c) % 4]))
    found.remove((0, 0, 0))
    return found


def peers():
    x, y, z, _ = coords()
    rows = [wrap(x + a) for a in range(4)]
    cols = [wrap(y + a) * 2 for a in range(4)]
    highs = [wrap(z + a) // 2 * 4 for a in range(4)]
    lows = [lax.rem(wrap(z + a), 2) for a in range(4)]
    return [(highs[c] + rows[a], cols[b] + lows[c]) for a, b, c in offsets()]


def greet(others, core, sibling):
    barrier = pltpu.get_barrier_semaphore()
    far = [sum((0, 1, 2, 1)[v] for v in offset) for offset in offsets()]
    for n in sorted(range(CHIPS - 1), key=lambda n: -far[n]):
        row, col = others[n]
        pl.semaphore_signal(
            barrier, inc=1, device_id=(row * 2 + core, col), device_id_type=MESH
        )
    pl.semaphore_signal(barrier, inc=1, device_id=sibling, device_id_type=MESH)


def wait_bytes(buffer, sem, count):
    part = buffer.at[pl.ds(0, count)]
    pltpu.make_async_copy(part, part, sem).wait()


def sigmoid(v):
    return 0.5 * jnp.tanh(0.5 * v) + 0.5


def normalise(values, gain):
    center = jnp.mean(values, axis=0, keepdims=True)
    moved = values - center
    spread = jnp.mean(moved * moved, axis=0, keepdims=True)
    return moved * lax.rsqrt(spread + EPSILON) * gain


def kernel(
    mask_hbm,
    pair_hbm,
    in_gain_hbm,
    proj_hbm,
    gate_hbm,
    out_gain_hbm,
    outw_hbm,
    out_hbm,
    out_ref,
    mask_ref,
    pair_ref,
    in_gain_ref,
    proj_ref,
    gate_ref,
    out_gain_ref,
    outw_ref,
    proj_t,
    outw_t,
    in_gain_t,
    out_gain_t,
    weight_of,
    state,
    gate,
    left_f,
    right_f,
    sides_s,
    sides_r,
    prod_s,
    prod_r,
    prod_f,
    left_m,
    left_k,
    right_m,
    in_sem,
    out_sem,
    over_send,
    over_recv,
    send_sem,
    recv_sem,
):
    row_index = lax.axis_index("row")
    col_index = lax.axis_index("col")
    core = lax.rem(row_index, 2)
    half_row = row_index // 2
    chip = half_row * 8 + col_index
    sibling = (half_row * 2 + 1 - core, col_index)
    others = peers()
    loads = [
        pltpu.make_async_copy(source, target, in_sem.at[n])
        for n, (source, target) in enumerate(
            (
                (mask_hbm, mask_ref),
                (proj_hbm, proj_ref),
                (gate_hbm, gate_ref),
                (in_gain_hbm, in_gain_ref),
                (pair_hbm, pair_ref),
                (out_gain_hbm, out_gain_ref),
                (outw_hbm, outw_ref),
            )
        )
    ]
    stores = [
        pltpu.make_async_copy(
            out_ref.at[pl.ds(part * 8 + h * HALF, 8)],
            out_hbm.at[pl.ds(part * 8 + h * HALF, 8)],
            out_sem.at[part * 2 + h],
        )
        for part in range(PARTS)
        for h in range(2)
    ]
    for load in loads:
        load.start()
    greet(others, core, sibling)

    def turn(u):
        for n in range(4):
            block = proj_ref[u, :, n * 128 : (n + 1) * 128].astype(jnp.float32)
            proj_t[u, n * 128 : (n + 1) * 128, :] = block.T.astype(jnp.bfloat16)
        proj_t[u, 512:640, :] = gate_ref[u].astype(jnp.float32).T.astype(jnp.bfloat16)
        in_gain_t[u] = jnp.broadcast_to(in_gain_ref[u : u + 1, :], (128, 128)).T

    def turn_out(u):
        outw_t[u] = outw_ref[u].astype(jnp.float32).T.astype(jnp.bfloat16)
        out_gain_t[u] = jnp.broadcast_to(out_gain_ref[u : u + 1, :], (128, 128)).T

    loads[0].wait()
    lane = lax.broadcasted_iota(jnp.int32, (8, 128), 1)
    low = lane < COLS
    lane_col = lax.rem(lane, COLS)
    col_flags = jnp.zeros((8, 128), jnp.float32)
    for j in range(COLS):
        flag = mask_ref[col_index * COLS + j].astype(jnp.float32)
        col_flags = jnp.where(lane_col == j, flag, col_flags)
    for t in range(TILES):
        upper = mask_ref[row_index * ROWS + t].astype(jnp.float32)
        lower = mask_ref[row_index * ROWS + HALF + t].astype(jnp.float32)
        weight_of[t // 2, :, t % 2 * 128 : t % 2 * 128 + 128] = col_flags * jnp.where(low, upper, lower)
    for n in (1, 2, 3):
        loads[n].wait()
    turn(0)
    loads[4].wait()

    def wide(column):
        return jnp.concatenate([column, column], axis=1)

    def project(u, p, values):
        normed = normalise(values, wide(in_gain_t[u])).astype(jnp.bfloat16)
        weight = weight_of[p][0:1, :]

        def times(n):
            return jnp.dot(
                proj_t[u, n * 128 : (n + 1) * 128, :], normed, preferred_element_type=jnp.float32
            )

        left = sigmoid(times(0)) * (times(1) * weight)
        right = sigmoid(times(2)) * (times(3) * weight)
        for j in range(2):
            left_f[pl.ds(p * 2 + j, C, stride=TILES), :] = left[:, j * 128 : j * 128 + 128]
            right_f[pl.ds(p * 2 + j, C, stride=TILES), :] = right[:, j * 128 : j * 128 + 128]
        gate[p] = sigmoid(times(4))

    def pack(u, part):
        def step(c, carry):
            at = pl.ds(pl.multiple_of(c * TILES + part * 8, 8), 8)
            both = jnp.concatenate([left_f[at, :], right_f[at, :]], axis=0)
            sides_s[u, part, c] = both.astype(jnp.bfloat16)
            return carry

        lax.fori_loop(0, C, step, 0, unroll=8)

    def channel(row, col, g):
        return (row * 2 + g) * 8 + col

    def send_sides(u, g, part):
        sem = (u * 2 + g) * 2 + part
        for row, col in others:
            pltpu.make_async_remote_copy(
                sides_s.at[u, part, channel(row, col, g)],
                sides_r.at[u, g, part, chip],
                send_sem.at[sem],
                recv_sem.at[sem],
                device_id=(row * 2 + core, col),
                device_id_type=MESH,
            ).start()
        sides_r[u, g, part, chip] = sides_s[u, part, channel(half_row, col_index, g)]

    def send_products(u, g):
        sem = 8 + u * 2 + g
        own = channel(half_row, col_index, g)
        for row, col in others:
            pltpu.make_async_remote_copy(
                prod_s.at[u, g, row * 8 + col],
                prod_r.at[u, own],
                send_sem.at[sem],
                recv_sem.at[sem],
                device_id=(row * 2 + core, col),
                device_id_type=MESH,
            ).start()
        prod_r[u, own] = prod_s[u, g, chip]

    def hand_over(buffer, sem):
        pltpu.make_async_remote_copy(
            buffer,
            buffer,
            over_send.at[sem],
            over_recv.at[sem],
            device_id=sibling,
            device_id_type=MESH,
        ).start()

    def first(p, carry):
        tiles = [
            jnp.concatenate([pair_ref[p * 2 + j], pair_ref[p * 2 + j + HALF]], axis=0)
            .astype(jnp.float32)
            .T
            for j in range(2)
        ]
        block = jnp.concatenate(tiles, axis=1)
        state[p] = block
        project(0, p, block)
        return carry

    lax.fori_loop(0, PAIRS // 2, first, 0, unroll=4)
    pack(0, 0)
    pl.semaphore_wait(pltpu.get_barrier_semaphore(), CHIPS)
    send_sides(0, 0, 0)
    lax.fori_loop(PAIRS // 2, PAIRS, first, 0, unroll=4)
    pack(0, 1)
    send_sides(0, 0, 1)
    send_sides(0, 1, 0)
    send_sides(0, 1, 1)
    for n in (5, 6):
        loads[n].wait()
    turn_out(0)
    turn(1)
    turn_out(1)

    def swap(a, b):
        one = jnp.where(low, a, pltpu.roll(b, COLS, 1))
        two = jnp.where(low, pltpu.roll(a, COLS, 1), b)
        return one, two

    def every(body):
        def step(q, carry):
            body(q)
            return carry

        lax.fori_loop(0, 8, step, 0, unroll=8)

    def turned_sides(u, g, part, q, m, side):
        tiles = [
            sides_r[u, g, part, q * 8 + 2 * m + j][side : side + 8, :].astype(jnp.float32)
            for j in range(2)
        ]
        return swap(tiles[0], tiles[1])

    for u in range(2):
        for g in range(2):
            for part in range(PARTS):
                wait_bytes(
                    sides_r.at[u, g, part], recv_sem.at[(u * 2 + g) * 2 + part], CHIPS - 1
                )

                def assemble(q):
                    for m in range(4):
                        across = slice(m * 128, (m + 1) * 128)
                        both = jnp.concatenate(turned_sides(u, g, part, q, m, 0), axis=0)
                        if u == 0:
                            at = pl.multiple_of(part * 128 + q * 16, 16)
                            left_m[g, pl.ds(at, 16), across] = both.astype(jnp.bfloat16)
                        else:
                            at = pl.multiple_of(part * 256 + core * 128 + q * 16, 16)
                            left_k[g, pl.ds(at, 16), across] = both.astype(jnp.bfloat16)
                            both = jnp.concatenate(turned_sides(u, g, part, q, m, 8), axis=0)
                            right_m[1, g, pl.ds(at, 16), across] = both.astype(jnp.bfloat16)

                every(assemble)
                if u == 1:
                    rows = pl.ds(pl.multiple_of(part * 256 + core * 128, 128), 128)
                    hand_over(left_k.at[g, rows], 2 + g * 4 + part * 2)
                    hand_over(right_m.at[1, g, rows], 3 + g * 4 + part * 2)
            if u == 0:

                def assemble_natural(q):
                    for m in range(4):
                        turned = [turned_sides(0, g, part, q, m, 8) for part in range(PARTS)]
                        for h in range(2):
                            both = jnp.concatenate([turned[0][h], turned[1][h]], axis=0)
                            at = pl.multiple_of((q * 2 + core) * ROWS + 16 * h, 16)
                            right_m[0, g, pl.ds(at, 16), m * 128 : (m + 1) * 128] = both.astype(
                                jnp.bfloat16
                            )

                every(assemble_natural)
                for q in range(8):
                    at = pl.multiple_of((q * 2 + core) * ROWS, ROWS)
                    hand_over(right_m.at[0, g, pl.ds(at, ROWS)], g)
                wait_bytes(right_m.at[0, g], over_recv.at[g], 256)
            else:
                for n in range(4):
                    wait_bytes(right_m.at[1, g], over_recv.at[2 + g * 4 + n], 128)

            def deliver(upper, lower, q, m):
                turned = [swap(upper[e], lower[e]) for e in range(2)]
                for h in range(2):
                    both = jnp.concatenate([turned[0][h], turned[1][h]], axis=0)
                    prod_s[u, g, q * 8 + 2 * m + h] = both.astype(jnp.bfloat16)

            if u == 0:
                for n in range(2):
                    rows = jnp.concatenate(
                        [
                            left_m[g, part * 128 + n * 64 : part * 128 + n * 64 + 64, :]
                            for part in range(2)
                        ],
                        axis=0,
                    )
                    product = lax.dot_general(
                        rows,
                        right_m[0, g],
                        (((1,), (1,)), ((), ())),
                        preferred_element_type=jnp.float32,
                    )
                    for q in range(4):
                        for m in range(4):
                            across = slice(m * 128, (m + 1) * 128)
                            upper, lower = (
                                [
                                    product[e * 64 + q * 16 + h * 8 :, across][:8]
                                    for e in range(2)
                                ]
                                for h in range(2)
                            )
                            deliver(upper, lower, n * 4 + q, m)
            else:
                first_core = core == 0
                for n in range(4):
                    product = lax.dot_general(
                        left_k[g, :, n * 128 : (n + 1) * 128],
                        right_m[1, g],
                        (((0,), (0,)), ((), ())),
                        preferred_element_type=jnp.float32,
                    )
                    for q in range(2):
                        for m in range(4):
                            across = slice(m * 128, (m + 1) * 128)
                            upper, lower = (
                                [
                                    jnp.where(
                                        first_core,
                                        product[q * 64 + h * 16 + e * 8 :, across][:8],
                                        product[q * 64 + 32 + h * 16 + e * 8 :, across][:8],
                                    )
                                    for e in range(2)
                                ]
                                for h in range(2)
                            )
                            deliver(upper, lower, n * 2 + q, m)
            send_products(u, g)

        for g in range(2):
            wait_bytes(prod_r.at[u], recv_sem.at[8 + u * 2 + g], CHIPS - 1)

            def unpack(q, carry):
                for col in range(8):
                    c = (q * 2 + g) * 8 + col
                    prod_f[pl.ds(pl.multiple_of(c * TILES, TILES), TILES), :] = prod_r[u, c].astype(
                        jnp.float32
                    )
                return carry

            lax.fori_loop(0, 8, unpack, 0)

        def finish(p, carry):
            product = jnp.concatenate(
                [prod_f[pl.ds(p * 2 + j, C, stride=TILES), :] for j in range(2)], axis=1
            )
            normout = normalise(product, wide(out_gain_t[u])).astype(jnp.bfloat16)
            update = jnp.dot(outw_t[u], normout, preferred_element_type=jnp.float32)
            new = (state[p] + gate[p] * update).astype(jnp.bfloat16).astype(jnp.float32)
            if u == 0:
                state[p] = new
            else:
                for j in range(2):
                    back = new[:, j * 128 : j * 128 + 128].T.astype(jnp.bfloat16)
                    out_ref[p * 2 + j] = back[0:COLS]
                    out_ref[p * 2 + j + HALF] = back[COLS : 2 * COLS]
            return carry

        def second(p, carry):
            project(1, p, state[p])
            return carry

        for part in range(PARTS):
            lax.fori_loop(part * 4, part * 4 + 4, finish, 0, unroll=4)
            if u == 0:
                lax.fori_loop(part * 4, part * 4 + 4, second, 0, unroll=4)
                pack(1, part)
                send_sides(1, 0, part)
            else:
                for h in range(2):
                    stores[part * 2 + h].start()
        if u == 0:
            for part in range(PARTS):
                send_sides(1, 1, part)

    for u in range(2):
        for g in range(2):
            for part in range(PARTS):
                sem = (u * 2 + g) * 2 + part
                wait_bytes(sides_r.at[u, g, part], send_sem.at[sem], CHIPS - 1)
            wait_bytes(prod_s.at[u, g], send_sem.at[8 + u * 2 + g], CHIPS - 1)
    for g in range(2):
        wait_bytes(right_m.at[0, g], over_send.at[g], 256)
        for n in range(4):
            wait_bytes(right_m.at[1, g], over_send.at[2 + g * 4 + n], 128)
    for store in stores:
        store.wait()


def shards(pair, residue_mask, in_gain, proj_weight, gate_weight, out_gain, out_weight):
    return pl.pallas_call(
        kernel,
        out_shape=jax.ShapeDtypeStruct(pair.shape, pair.dtype),
        in_specs=[pl.BlockSpec(memory_space=pl.ANY)] * 7,
        out_specs=pl.BlockSpec(memory_space=pl.ANY),
        scratch_shapes=[
            pltpu.VMEM(pair.shape, pair.dtype),
            pltpu.SMEM(residue_mask.shape, residue_mask.dtype),
            pltpu.VMEM(pair.shape, pair.dtype),
            pltpu.VMEM(in_gain.shape, in_gain.dtype),
            pltpu.VMEM(proj_weight.shape, proj_weight.dtype),
            pltpu.VMEM(gate_weight.shape, gate_weight.dtype),
            pltpu.VMEM(out_gain.shape, out_gain.dtype),
            pltpu.VMEM(out_weight.shape, out_weight.dtype),
            pltpu.VMEM((2, 640, 128), jnp.bfloat16),
            pltpu.VMEM((2, 128, 128), jnp.bfloat16),
            pltpu.VMEM((2, 128, 128), jnp.float32),
            pltpu.VMEM((2, 128, 128), jnp.float32),
            pltpu.VMEM((PAIRS, 8, 256), jnp.float32),
            pltpu.VMEM((PAIRS, 128, 256), jnp.float32),
            pltpu.VMEM((PAIRS, 128, 256), jnp.float32),
            pltpu.VMEM((C * TILES, 128), jnp.float32),
            pltpu.VMEM((C * TILES, 128), jnp.float32),
            pltpu.VMEM((2, PARTS, C, 16, 128), jnp.bfloat16),
            pltpu.VMEM((2, 2, PARTS, CHIPS, 16, 128), jnp.bfloat16),
            pltpu.VMEM((2, 2, CHIPS, 16, 128), jnp.bfloat16),
            pltpu.VMEM((2, C, 16, 128), jnp.bfloat16),
            pltpu.VMEM((C * TILES, 128), jnp.float32),
            pltpu.VMEM((2, 256, 512), jnp.bfloat16),
            pltpu.VMEM((2, 512, 512), jnp.bfloat16),
            pltpu.VMEM((2, 2, 512, 512), jnp.bfloat16),
            pltpu.SemaphoreType.DMA((7,)),
            pltpu.SemaphoreType.DMA((4,)),
            pltpu.SemaphoreType.DMA((10,)),
            pltpu.SemaphoreType.DMA((10,)),
            pltpu.SemaphoreType.DMA((12,)),
            pltpu.SemaphoreType.DMA((12,)),
        ],
        compiler_params=pltpu.CompilerParams(
            collective_id=0, has_side_effects=True, vmem_limit_bytes=58 * 1024 * 1024
        ),
    )(residue_mask, pair, in_gain, proj_weight, gate_weight, out_gain, out_weight)


def solution(mesh):
    placed = (P("row", "col", None), P(), P(), P(), P(), P(), P())
    return jax.shard_map(
        shards, mesh=mesh, in_specs=placed, out_specs=P("row", "col", None), check_vma=False
    )
```

```python
import jax
import jax.numpy as jnp
from jax import lax
from jax.experimental import pallas as pl
from jax.experimental.pallas import tpu as pltpu
from jax.sharding import PartitionSpec as P

EPSILON = 1e-05
MESH = pl.DeviceIdType.MESH
CHIPS = 64
C = 128
ROWS = 32
COLS = 64
HALF = ROWS // 2
TILES = 16
PAIRS = 8
PARTS = 2


def coords():
    r = lax.axis_index("row")
    c = lax.axis_index("col")
    return lax.rem(r // 2, 4), c // 2, (r // 8) * 2 + lax.rem(c, 2), lax.rem(r, 2)


def device_at(x, y, z, k):
    return ((z // 2) * 8 + x * 2 + k, y * 2 + lax.rem(z, 2))


def wrap(a):
    return lax.rem(a + 4, 4)


def offsets():
    far = (2, 1, 3, 0)
    found = []
    for s in range(CHIPS):
        a, b, c = s % 4, s // 4 % 4, s // 16
        found.append((far[a], far[(a + b) % 4], far[(a + b + c) % 4]))
    found.remove((0, 0, 0))
    return sorted(found, key=lambda offset: -sum((0, 1, 2, 1)[v] for v in offset))


def peers():
    x, y, z, _ = coords()
    rows = [wrap(x + a) for a in range(4)]
    cols = [wrap(y + a) * 2 for a in range(4)]
    highs = [wrap(z + a) // 2 * 4 for a in range(4)]
    lows = [lax.rem(wrap(z + a), 2) for a in range(4)]
    return [(highs[c] + rows[a], cols[b] + lows[c]) for a, b, c in offsets()]


def greet(others, core, sibling):
    barrier = pltpu.get_barrier_semaphore()
    for row, col in others:
        pl.semaphore_signal(
            barrier, inc=1, device_id=(row * 2 + core, col), device_id_type=MESH
        )
    pl.semaphore_signal(barrier, inc=1, device_id=sibling, device_id_type=MESH)


def wait_bytes(buffer, sem, count):
    part = buffer.at[pl.ds(0, count)]
    pltpu.make_async_copy(part, part, sem).wait()


def sigmoid(v):
    return 0.5 * jnp.tanh(0.5 * v) + 0.5


def normalise(values, gain):
    center = jnp.mean(values, axis=0, keepdims=True)
    moved = values - center
    spread = jnp.mean(moved * moved, axis=0, keepdims=True)
    return moved * lax.rsqrt(spread + EPSILON) * gain


def kernel(
    mask_hbm,
    pair_hbm,
    in_gain_hbm,
    proj_hbm,
    gate_hbm,
    out_gain_hbm,
    outw_hbm,
    out_hbm,
    out_ref,
    mask_ref,
    pair_ref,
    in_gain_ref,
    proj_ref,
    gate_ref,
    out_gain_ref,
    outw_ref,
    proj_t,
    outw_t,
    in_gain_t,
    out_gain_t,
    weight_of,
    state,
    gate,
    left_f,
    right_f,
    sides_s,
    sides_r,
    prod_s,
    prod_r,
    prod_f,
    left_m,
    left_k,
    right_m,
    own_sum,
    in_sem,
    out_sem,
    over_send,
    over_recv,
    send_sem,
    recv_sem,
):
    row_index = lax.axis_index("row")
    col_index = lax.axis_index("col")
    core = lax.rem(row_index, 2)
    half_row = row_index // 2
    chip = half_row * 8 + col_index
    sibling = (half_row * 2 + 1 - core, col_index)
    others = peers()
    loads = [
        pltpu.make_async_copy(source, target, in_sem.at[n])
        for n, (source, target) in enumerate(
            (
                (mask_hbm, mask_ref),
                (proj_hbm, proj_ref),
                (gate_hbm, gate_ref),
                (in_gain_hbm, in_gain_ref),
                (pair_hbm, pair_ref),
                (out_gain_hbm, out_gain_ref),
                (outw_hbm, outw_ref),
            )
        )
    ]
    stores = [
        pltpu.make_async_copy(
            out_ref.at[pl.ds(part * 8 + h * HALF, 8)],
            out_hbm.at[pl.ds(part * 8 + h * HALF, 8)],
            out_sem.at[part * 2 + h],
        )
        for part in range(PARTS)
        for h in range(2)
    ]
    for load in loads:
        load.start()
    greet(others, core, sibling)

    def turn(u):
        for n in range(4):
            block = proj_ref[u, :, n * 128 : (n + 1) * 128].astype(jnp.float32)
            proj_t[u, n * 128 : (n + 1) * 128, :] = block.T.astype(jnp.bfloat16)
        proj_t[u, 512:640, :] = gate_ref[u].astype(jnp.float32).T.astype(jnp.bfloat16)
        in_gain_t[u] = jnp.broadcast_to(in_gain_ref[u : u + 1, :], (128, 128)).T

    def turn_out(u):
        outw_t[u] = outw_ref[u].astype(jnp.float32).T.astype(jnp.bfloat16)
        out_gain_t[u] = jnp.broadcast_to(out_gain_ref[u : u + 1, :], (128, 128)).T

    loads[0].wait()
    lane = lax.broadcasted_iota(jnp.int32, (8, 128), 1)
    low = lane < COLS
    lane_col = lax.rem(lane, COLS)
    col_flags = jnp.zeros((8, 128), jnp.float32)
    for j in range(COLS):
        flag = mask_ref[col_index * COLS + j].astype(jnp.float32)
        col_flags = jnp.where(lane_col == j, flag, col_flags)
    for t in range(TILES):
        upper = mask_ref[row_index * ROWS + t].astype(jnp.float32)
        lower = mask_ref[row_index * ROWS + HALF + t].astype(jnp.float32)
        weight_of[t // 2, :, t % 2 * 128 : t % 2 * 128 + 128] = col_flags * jnp.where(low, upper, lower)
    for n in (1, 2, 3):
        loads[n].wait()
    turn(0)
    loads[4].wait()

    def wide(column):
        return jnp.concatenate([column, column], axis=1)

    def project(u, p, values):
        normed = normalise(values, wide(in_gain_t[u])).astype(jnp.bfloat16)
        weight = weight_of[p][0:1, :]

        def times(n):
            return jnp.dot(
                proj_t[u, n * 128 : (n + 1) * 128, :], normed, preferred_element_type=jnp.float32
            )

        left = sigmoid(times(0)) * (times(1) * weight)
        right = sigmoid(times(2)) * (times(3) * weight)
        for j in range(2):
            left_f[pl.ds(p * 2 + j, C, stride=TILES), :] = left[:, j * 128 : j * 128 + 128]
            right_f[pl.ds(p * 2 + j, C, stride=TILES), :] = right[:, j * 128 : j * 128 + 128]
        gate[p] = sigmoid(times(4))

    def pack(u, part, g):
        def step(row, carry):
            for col in range(8):
                c = channel(row, col, g)
                at = pl.ds(pl.multiple_of(c * TILES + part * 8, 8), 8)
                both = jnp.concatenate([left_f[at, :], right_f[at, :]], axis=0)
                sides_s[u, part, c] = both.astype(jnp.bfloat16)
            return carry

        lax.fori_loop(0, 8, step, 0, unroll=4)

    def channel(row, col, g):
        return (row * 2 + g) * 8 + col

    def send_sides(u, g, part):
        sem = (u * 2 + g) * 2 + part
        for row, col in others:
            pltpu.make_async_remote_copy(
                sides_s.at[u, part, channel(row, col, g)],
                sides_r.at[u, g, part, chip],
                send_sem.at[sem],
                recv_sem.at[sem],
                device_id=(row * 2 + core, col),
                device_id_type=MESH,
            ).start()
        sides_r[u, g, part, chip] = sides_s[u, part, channel(half_row, col_index, g)]

    def send_products(u, g):
        sem = 8 + u * 2 + g
        own = channel(half_row, col_index, g)
        for row, col in others[::-1] if g == 0 else others:
            pltpu.make_async_remote_copy(
                prod_s.at[u, g, row * 8 + col],
                prod_r.at[u, own],
                send_sem.at[sem],
                recv_sem.at[sem],
                device_id=(row * 2 + core, col),
                device_id_type=MESH,
            ).start()
        prod_r[u, own] = prod_s[u, g, chip]

    def hand_over(buffer, sem):
        pltpu.make_async_remote_copy(
            buffer,
            buffer,
            over_send.at[sem],
            over_recv.at[sem],
            device_id=sibling,
            device_id_type=MESH,
        ).start()

    def first(p, carry):
        tiles = [
            jnp.concatenate([pair_ref[p * 2 + j], pair_ref[p * 2 + j + HALF]], axis=0)
            .astype(jnp.float32)
            .T
            for j in range(2)
        ]
        block = jnp.concatenate(tiles, axis=1)
        state[p] = block
        project(0, p, block)
        return carry

    lax.fori_loop(0, PAIRS // 2, first, 0, unroll=4)
    pack(0, 0, 0)
    pl.semaphore_wait(pltpu.get_barrier_semaphore(), CHIPS)
    send_sides(0, 0, 0)
    lax.fori_loop(PAIRS // 2, PAIRS, first, 0, unroll=4)
    pack(0, 1, 0)
    send_sides(0, 0, 1)
    for part in range(PARTS):
        pack(0, part, 1)
        send_sides(0, 1, part)
    for n in (5, 6):
        loads[n].wait()
    turn_out(0)
    turn(1)
    turn_out(1)

    def swap(a, b):
        one = jnp.where(low, a, pltpu.roll(b, COLS, 1))
        two = jnp.where(low, pltpu.roll(a, COLS, 1), b)
        return one, two

    def every(body):
        def step(q, carry):
            body(q)
            return carry

        lax.fori_loop(0, 8, step, 0, unroll=8)

    def turned_sides(u, g, part, q, m, side):
        tiles = [
            sides_r[u, g, part, q * 8 + 2 * m + j][side : side + 8, :].astype(jnp.float32)
            for j in range(2)
        ]
        return swap(tiles[0], tiles[1])

    for u in range(2):
        for g in range(2):
            for part in range(PARTS):
                wait_bytes(
                    sides_r.at[u, g, part], recv_sem.at[(u * 2 + g) * 2 + part], CHIPS - 1
                )

                def assemble(q):
                    for m in range(4):
                        across = slice(m * 128, (m + 1) * 128)
                        both = jnp.concatenate(turned_sides(u, g, part, q, m, 0), axis=0)
                        if u == 0:
                            at = pl.multiple_of(part * 128 + q * 16, 16)
                            left_m[g, pl.ds(at, 16), across] = both.astype(jnp.bfloat16)
                        else:
                            at = pl.multiple_of(core * 256 + part * 128 + q * 16, 16)
                            left_k[g, pl.ds(at, 16), across] = both.astype(jnp.bfloat16)
                            both = jnp.concatenate(turned_sides(u, g, part, q, m, 8), axis=0)
                            right_m[1, g, pl.ds(at, 16), across] = both.astype(jnp.bfloat16)

                every(assemble)
                if u == 1:
                    rows = pl.ds(pl.multiple_of(core * 256 + part * 128, 128), 128)
                    hand_over(left_k.at[g, rows], 2 + g * 4 + part * 2)
                    hand_over(right_m.at[1, g, rows], 3 + g * 4 + part * 2)
            if u == 0:

                def assemble_natural(q):
                    for m in range(4):
                        turned = [turned_sides(0, g, part, q, m, 8) for part in range(PARTS)]
                        for h in range(2):
                            both = jnp.concatenate([turned[0][h], turned[1][h]], axis=0)
                            at = pl.multiple_of((q * 2 + core) * ROWS + 16 * h, 16)
                            right_m[0, g, pl.ds(at, 16), m * 128 : (m + 1) * 128] = both.astype(
                                jnp.bfloat16
                            )

                every(assemble_natural)
                for q in range(8):
                    at = pl.multiple_of((q * 2 + core) * ROWS, ROWS)
                    hand_over(right_m.at[0, g, pl.ds(at, ROWS)], g)
                wait_bytes(right_m.at[0, g], over_recv.at[g], 256)
            else:

                def half_product(n, which):
                    rows = pl.ds(pl.multiple_of(which * 256, 256), 256)
                    return lax.dot_general(
                        left_k[g, rows, n * 128 : (n + 1) * 128],
                        right_m[1, g, rows, :],
                        (((0,), (0,)), ((), ())),
                        preferred_element_type=jnp.float32,
                    )

                for n in range(4):
                    own_sum[n] = half_product(n, core)
                for n in range(4):
                    wait_bytes(right_m.at[1, g], over_recv.at[2 + g * 4 + n], 128)

            def deliver(upper, lower, q, m):
                turned = [swap(upper[e], lower[e]) for e in range(2)]
                for h in range(2):
                    both = jnp.concatenate([turned[0][h], turned[1][h]], axis=0)
                    prod_s[u, g, q * 8 + 2 * m + h] = both.astype(jnp.bfloat16)

            if u == 0:
                for n in range(2):
                    rows = jnp.concatenate(
                        [
                            left_m[g, part * 128 + n * 64 : part * 128 + n * 64 + 64, :]
                            for part in range(2)
                        ],
                        axis=0,
                    )
                    product = lax.dot_general(
                        rows,
                        right_m[0, g],
                        (((1,), (1,)), ((), ())),
                        preferred_element_type=jnp.float32,
                    )
                    for q in range(4):
                        for m in range(4):
                            across = slice(m * 128, (m + 1) * 128)
                            upper, lower = (
                                [
                                    product[e * 64 + q * 16 + h * 8 :, across][:8]
                                    for e in range(2)
                                ]
                                for h in range(2)
                            )
                            deliver(upper, lower, n * 4 + q, m)
            else:
                first_core = core == 0
                for n in range(4):
                    product = own_sum[n] + half_product(n, 1 - core)
                    for q in range(2):
                        for m in range(4):
                            across = slice(m * 128, (m + 1) * 128)
                            upper, lower = (
                                [
                                    jnp.where(
                                        first_core,
                                        product[q * 64 + h * 16 + e * 8 :, across][:8],
                                        product[q * 64 + 32 + h * 16 + e * 8 :, across][:8],
                                    )
                                    for e in range(2)
                                ]
                                for h in range(2)
                            )
                            deliver(upper, lower, n * 2 + q, m)
            send_products(u, g)

        for g in range(2):
            wait_bytes(prod_r.at[u], recv_sem.at[8 + u * 2 + g], CHIPS - 1)

            def unpack(q, carry):
                for col in range(8):
                    c = (q * 2 + g) * 8 + col
                    prod_f[pl.ds(pl.multiple_of(c * TILES, TILES), TILES), :] = prod_r[u, c].astype(
                        jnp.float32
                    )
                return carry

            lax.fori_loop(0, 8, unpack, 0)

        def finish(p, carry):
            product = jnp.concatenate(
                [prod_f[pl.ds(p * 2 + j, C, stride=TILES), :] for j in range(2)], axis=1
            )
            normout = normalise(product, wide(out_gain_t[u])).astype(jnp.bfloat16)
            update = jnp.dot(outw_t[u], normout, preferred_element_type=jnp.float32)
            new = (state[p] + gate[p] * update).astype(jnp.bfloat16).astype(jnp.float32)
            if u == 0:
                state[p] = new
            else:
                for j in range(2):
                    back = new[:, j * 128 : j * 128 + 128].T.astype(jnp.bfloat16)
                    out_ref[p * 2 + j] = back[0:COLS]
                    out_ref[p * 2 + j + HALF] = back[COLS : 2 * COLS]
            return carry

        def second(p, carry):
            project(1, p, state[p])
            return carry

        for part in range(PARTS):
            lax.fori_loop(part * 4, part * 4 + 4, finish, 0, unroll=4)
            if u == 0:
                lax.fori_loop(part * 4, part * 4 + 4, second, 0, unroll=4)
                pack(1, part, 0)
                send_sides(1, 0, part)
            else:
                for h in range(2):
                    stores[part * 2 + h].start()
        if u == 0:
            for part in range(PARTS):
                pack(1, part, 1)
                send_sides(1, 1, part)

    for u in range(2):
        for g in range(2):
            for part in range(PARTS):
                sem = (u * 2 + g) * 2 + part
                wait_bytes(sides_r.at[u, g, part], send_sem.at[sem], CHIPS - 1)
            wait_bytes(prod_s.at[u, g], send_sem.at[8 + u * 2 + g], CHIPS - 1)
    for g in range(2):
        wait_bytes(right_m.at[0, g], over_send.at[g], 256)
        for n in range(4):
            wait_bytes(right_m.at[1, g], over_send.at[2 + g * 4 + n], 128)
    for store in stores:
        store.wait()


def shards(pair, residue_mask, in_gain, proj_weight, gate_weight, out_gain, out_weight):
    return pl.pallas_call(
        kernel,
        out_shape=jax.ShapeDtypeStruct(pair.shape, pair.dtype),
        in_specs=[pl.BlockSpec(memory_space=pl.ANY)] * 7,
        out_specs=pl.BlockSpec(memory_space=pl.ANY),
        scratch_shapes=[
            pltpu.VMEM(pair.shape, pair.dtype),
            pltpu.SMEM(residue_mask.shape, residue_mask.dtype),
            pltpu.VMEM(pair.shape, pair.dtype),
            pltpu.VMEM(in_gain.shape, in_gain.dtype),
            pltpu.VMEM(proj_weight.shape, proj_weight.dtype),
            pltpu.VMEM(gate_weight.shape, gate_weight.dtype),
            pltpu.VMEM(out_gain.shape, out_gain.dtype),
            pltpu.VMEM(out_weight.shape, out_weight.dtype),
            pltpu.VMEM((2, 640, 128), jnp.bfloat16),
            pltpu.VMEM((2, 128, 128), jnp.bfloat16),
            pltpu.VMEM((2, 128, 128), jnp.float32),
            pltpu.VMEM((2, 128, 128), jnp.float32),
            pltpu.VMEM((PAIRS, 8, 256), jnp.float32),
            pltpu.VMEM((PAIRS, 128, 256), jnp.float32),
            pltpu.VMEM((PAIRS, 128, 256), jnp.float32),
            pltpu.VMEM((C * TILES, 128), jnp.float32),
            pltpu.VMEM((C * TILES, 128), jnp.float32),
            pltpu.VMEM((2, PARTS, C, 16, 128), jnp.bfloat16),
            pltpu.VMEM((2, 2, PARTS, CHIPS, 16, 128), jnp.bfloat16),
            pltpu.VMEM((2, 2, CHIPS, 16, 128), jnp.bfloat16),
            pltpu.VMEM((2, C, 16, 128), jnp.bfloat16),
            pltpu.VMEM((C * TILES, 128), jnp.float32),
            pltpu.VMEM((2, 256, 512), jnp.bfloat16),
            pltpu.VMEM((2, 512, 512), jnp.bfloat16),
            pltpu.VMEM((2, 2, 512, 512), jnp.bfloat16),
            pltpu.VMEM((4, 128, 512), jnp.float32),
            pltpu.SemaphoreType.DMA((7,)),
            pltpu.SemaphoreType.DMA((4,)),
            pltpu.SemaphoreType.DMA((10,)),
            pltpu.SemaphoreType.DMA((10,)),
            pltpu.SemaphoreType.DMA((12,)),
            pltpu.SemaphoreType.DMA((12,)),
        ],
        compiler_params=pltpu.CompilerParams(
            collective_id=0, has_side_effects=True, vmem_limit_bytes=58 * 1024 * 1024
        ),
    )(residue_mask, pair, in_gain, proj_weight, gate_weight, out_gain, out_weight)


def solution(mesh):
    placed = (P("row", "col", None), P(), P(), P(), P(), P(), P())
    return jax.shard_map(
        shards, mesh=mesh, in_specs=placed, out_specs=P("row", "col", None), check_vma=False
    )
```

```python
import jax
import jax.numpy as jnp
from jax import lax
from jax.experimental import pallas as pl
from jax.experimental.pallas import tpu as pltpu
from jax.sharding import PartitionSpec as P

EPSILON = 1e-05
MESH = pl.DeviceIdType.MESH
CHIPS = 64
C = 128
ROWS = 32
COLS = 64
HALF = ROWS // 2
TILES = 16
PAIRS = 8
PARTS = 2


def coords():
    r = lax.axis_index("row")
    c = lax.axis_index("col")
    return lax.rem(r // 2, 4), c // 2, (r // 8) * 2 + lax.rem(c, 2), lax.rem(r, 2)


def device_at(x, y, z, k):
    return ((z // 2) * 8 + x * 2 + k, y * 2 + lax.rem(z, 2))


def wrap(a):
    return lax.rem(a + 4, 4)


def offsets():
    far = (2, 1, 3, 0)
    found = []
    for s in range(CHIPS):
        a, b, c = s % 4, s // 4 % 4, s // 16
        found.append((far[a], far[(a + b) % 4], far[(a + b + c) % 4]))
    found.remove((0, 0, 0))
    return sorted(found, key=lambda offset: -sum((0, 1, 2, 1)[v] for v in offset))


def peers():
    x, y, z, _ = coords()
    rows = [wrap(x + a) for a in range(4)]
    cols = [wrap(y + a) * 2 for a in range(4)]
    highs = [wrap(z + a) // 2 * 4 for a in range(4)]
    lows = [lax.rem(wrap(z + a), 2) for a in range(4)]
    return [(highs[c] + rows[a], cols[b] + lows[c]) for a, b, c in offsets()]


def greet(others, core, sibling):
    barrier = pltpu.get_barrier_semaphore()
    for row, col in others:
        pl.semaphore_signal(
            barrier, inc=1, device_id=(row * 2 + core, col), device_id_type=MESH
        )
    pl.semaphore_signal(barrier, inc=1, device_id=sibling, device_id_type=MESH)


def wait_bytes(buffer, sem, count):
    part = buffer.at[pl.ds(0, count)]
    pltpu.make_async_copy(part, part, sem).wait()


def sigmoid(v):
    return 0.5 * jnp.tanh(0.5 * v) + 0.5


def normalise(values, gain):
    center = jnp.mean(values, axis=0, keepdims=True)
    moved = values - center
    spread = jnp.mean(moved * moved, axis=0, keepdims=True)
    return moved * lax.rsqrt(spread + EPSILON) * gain


def kernel(
    mask_hbm,
    pair_hbm,
    in_gain_hbm,
    proj_hbm,
    gate_hbm,
    out_gain_hbm,
    outw_hbm,
    out_hbm,
    out_ref,
    mask_ref,
    pair_ref,
    in_gain_ref,
    proj_ref,
    gate_ref,
    out_gain_ref,
    outw_ref,
    proj_t,
    outw_t,
    in_gain_t,
    out_gain_t,
    weight_of,
    state,
    gate,
    left_f,
    right_f,
    sides_s,
    sides_r,
    prod_s,
    prod_r,
    prod_f,
    left_m,
    left_k,
    right_m,
    own_sum,
    in_sem,
    out_sem,
    over_send,
    over_recv,
    send_sem,
    recv_sem,
):
    row_index = lax.axis_index("row")
    col_index = lax.axis_index("col")
    core = lax.rem(row_index, 2)
    half_row = row_index // 2
    chip = half_row * 8 + col_index
    sibling = (half_row * 2 + 1 - core, col_index)
    others = peers()
    loads = [
        pltpu.make_async_copy(source, target, in_sem.at[n])
        for n, (source, target) in enumerate(
            (
                (mask_hbm, mask_ref),
                (proj_hbm, proj_ref),
                (gate_hbm, gate_ref),
                (in_gain_hbm, in_gain_ref),
                (pair_hbm, pair_ref),
                (out_gain_hbm, out_gain_ref),
                (outw_hbm, outw_ref),
            )
        )
    ]
    stores = [
        pltpu.make_async_copy(
            out_ref.at[pl.ds(part * 8 + h * HALF, 8)],
            out_hbm.at[pl.ds(part * 8 + h * HALF, 8)],
            out_sem.at[part * 2 + h],
        )
        for part in range(PARTS)
        for h in range(2)
    ]
    for load in loads:
        load.start()
    greet(others, core, sibling)

    def turn(u):
        for n in range(4):
            block = proj_ref[u, :, n * 128 : (n + 1) * 128].astype(jnp.float32)
            proj_t[u, n * 128 : (n + 1) * 128, :] = block.T.astype(jnp.bfloat16)
        proj_t[u, 512:640, :] = gate_ref[u].astype(jnp.float32).T.astype(jnp.bfloat16)
        in_gain_t[u] = jnp.broadcast_to(in_gain_ref[u : u + 1, :], (128, 128)).T

    def turn_out(u):
        outw_t[u] = outw_ref[u].astype(jnp.float32).T.astype(jnp.bfloat16)
        out_gain_t[u] = jnp.broadcast_to(out_gain_ref[u : u + 1, :], (128, 128)).T

    loads[0].wait()
    lane = lax.broadcasted_iota(jnp.int32, (8, 128), 1)
    low = lane < COLS
    lane_col = lax.rem(lane, COLS)
    col_flags = jnp.zeros((8, 128), jnp.float32)
    for j in range(COLS):
        flag = mask_ref[col_index * COLS + j].astype(jnp.float32)
        col_flags = jnp.where(lane_col == j, flag, col_flags)
    for t in range(TILES):
        upper = mask_ref[row_index * ROWS + t].astype(jnp.float32)
        lower = mask_ref[row_index * ROWS + HALF + t].astype(jnp.float32)
        weight_of[t // 2, :, t % 2 * 128 : t % 2 * 128 + 128] = col_flags * jnp.where(low, upper, lower)
    for n in (1, 2, 3):
        loads[n].wait()
    turn(0)
    loads[4].wait()

    def wide(column):
        return jnp.concatenate([column, column], axis=1)

    def project(u, p, values):
        normed = normalise(values, wide(in_gain_t[u])).astype(jnp.bfloat16)
        weight = weight_of[p][0:1, :]

        def times(n):
            return jnp.dot(
                proj_t[u, n * 128 : (n + 1) * 128, :], normed, preferred_element_type=jnp.float32
            )

        left = sigmoid(times(0)) * (times(1) * weight)
        right = sigmoid(times(2)) * (times(3) * weight)
        for j in range(2):
            left_f[pl.ds(p * 2 + j, C, stride=TILES), :] = left[:, j * 128 : j * 128 + 128]
            right_f[pl.ds(p * 2 + j, C, stride=TILES), :] = right[:, j * 128 : j * 128 + 128]
        gate[p] = sigmoid(times(4))

    def pack(u, part, g):
        def step(row, carry):
            for col in range(8):
                c = channel(row, col, g)
                at = pl.ds(pl.multiple_of(c * TILES + part * 8, 8), 8)
                both = jnp.concatenate([left_f[at, :], right_f[at, :]], axis=0)
                sides_s[u, c, part] = both.astype(jnp.bfloat16)
            return carry

        lax.fori_loop(0, 8, step, 0, unroll=4)

    def channel(row, col, g):
        return (row * 2 + g) * 8 + col

    def send_sides(u, g, part):
        sem = (u * 2 + g) * 2 + part
        at = slice(None) if g == 1 else part
        for row, col in others:
            pltpu.make_async_remote_copy(
                sides_s.at[u, channel(row, col, g), at],
                sides_r.at[u, g, chip, at],
                send_sem.at[sem],
                recv_sem.at[sem],
                device_id=(row * 2 + core, col),
                device_id_type=MESH,
            ).start()
        sides_r[u, g, chip, at] = sides_s[u, channel(half_row, col_index, g), at]

    def send_products(u, g):
        sem = 8 + u * 2 + g
        own = channel(half_row, col_index, g)
        for row, col in others[::-1] if g == 0 else others:
            pltpu.make_async_remote_copy(
                prod_s.at[u, g, row * 8 + col],
                prod_r.at[u, own],
                send_sem.at[sem],
                recv_sem.at[sem],
                device_id=(row * 2 + core, col),
                device_id_type=MESH,
            ).start()
        prod_r[u, own] = prod_s[u, g, chip]

    def hand_over(buffer, sem):
        pltpu.make_async_remote_copy(
            buffer,
            buffer,
            over_send.at[sem],
            over_recv.at[sem],
            device_id=sibling,
            device_id_type=MESH,
        ).start()

    def first(p, carry):
        tiles = [
            jnp.concatenate([pair_ref[p * 2 + j], pair_ref[p * 2 + j + HALF]], axis=0)
            .astype(jnp.float32)
            .T
            for j in range(2)
        ]
        block = jnp.concatenate(tiles, axis=1)
        state[p] = block
        project(0, p, block)
        return carry

    lax.fori_loop(0, PAIRS // 2, first, 0, unroll=4)
    pack(0, 0, 0)
    pl.semaphore_wait(pltpu.get_barrier_semaphore(), CHIPS)
    send_sides(0, 0, 0)
    lax.fori_loop(PAIRS // 2, PAIRS, first, 0, unroll=4)
    pack(0, 1, 0)
    send_sides(0, 0, 1)
    for part in range(PARTS):
        pack(0, part, 1)
    send_sides(0, 1, 0)
    for n in (5, 6):
        loads[n].wait()
    turn_out(0)
    turn(1)
    turn_out(1)

    def swap(a, b):
        one = jnp.where(low, a, pltpu.roll(b, COLS, 1))
        two = jnp.where(low, pltpu.roll(a, COLS, 1), b)
        return one, two

    def every(body):
        def step(q, carry):
            body(q)
            return carry

        lax.fori_loop(0, 8, step, 0, unroll=8)

    def turned_sides(u, g, part, q, m, side):
        tiles = [
            sides_r[u, g, q * 8 + 2 * m + j, part][side : side + 8, :].astype(jnp.float32)
            for j in range(2)
        ]
        return swap(tiles[0], tiles[1])

    for u in range(2):
        for g in range(2):
            for part in range(PARTS):
                if g == 0:
                    wait_bytes(prod_r.at[u], recv_sem.at[u * 4 + part], CHIPS - 1)
                elif part == 0:
                    wait_bytes(sides_r.at[u, g], recv_sem.at[u * 4 + 2], CHIPS - 1)

                def assemble(q):
                    for m in range(4):
                        across = slice(m * 128, (m + 1) * 128)
                        both = jnp.concatenate(turned_sides(u, g, part, q, m, 0), axis=0)
                        if u == 0:
                            at = pl.multiple_of(part * 128 + q * 16, 16)
                            left_m[g, pl.ds(at, 16), across] = both.astype(jnp.bfloat16)
                        else:
                            at = pl.multiple_of(core * 256 + part * 128 + q * 16, 16)
                            left_k[g, pl.ds(at, 16), across] = both.astype(jnp.bfloat16)
                            both = jnp.concatenate(turned_sides(u, g, part, q, m, 8), axis=0)
                            right_m[1, g, pl.ds(at, 16), across] = both.astype(jnp.bfloat16)

                every(assemble)
                if u == 1:
                    rows = pl.ds(pl.multiple_of(core * 256 + part * 128, 128), 128)
                    hand_over(left_k.at[g, rows], 2 + g * 4 + part * 2)
                    hand_over(right_m.at[1, g, rows], 3 + g * 4 + part * 2)
            if u == 0:

                def assemble_natural(q):
                    for m in range(4):
                        turned = [turned_sides(0, g, part, q, m, 8) for part in range(PARTS)]
                        for h in range(2):
                            both = jnp.concatenate([turned[0][h], turned[1][h]], axis=0)
                            at = pl.multiple_of((q * 2 + core) * ROWS + 16 * h, 16)
                            right_m[0, g, pl.ds(at, 16), m * 128 : (m + 1) * 128] = both.astype(
                                jnp.bfloat16
                            )

                every(assemble_natural)
                for q in range(8):
                    at = pl.multiple_of((q * 2 + core) * ROWS, ROWS)
                    hand_over(right_m.at[0, g, pl.ds(at, ROWS)], g)
                wait_bytes(right_m.at[0, g], over_recv.at[g], 256)
            else:

                def half_product(n, which):
                    rows = pl.ds(pl.multiple_of(which * 256, 256), 256)
                    return lax.dot_general(
                        left_k[g, rows, n * 128 : (n + 1) * 128],
                        right_m[1, g, rows, :],
                        (((0,), (0,)), ((), ())),
                        preferred_element_type=jnp.float32,
                    )

                for n in range(4):
                    own_sum[n] = half_product(n, core)
                for n in range(4):
                    wait_bytes(right_m.at[1, g], over_recv.at[2 + g * 4 + n], 128)

            def deliver(upper, lower, q, m):
                turned = [swap(upper[e], lower[e]) for e in range(2)]
                for h in range(2):
                    both = jnp.concatenate([turned[0][h], turned[1][h]], axis=0)
                    prod_s[u, g, q * 8 + 2 * m + h] = both.astype(jnp.bfloat16)

            if u == 0:
                for n in range(2):
                    rows = jnp.concatenate(
                        [
                            left_m[g, part * 128 + n * 64 : part * 128 + n * 64 + 64, :]
                            for part in range(2)
                        ],
                        axis=0,
                    )
                    product = lax.dot_general(
                        rows,
                        right_m[0, g],
                        (((1,), (1,)), ((), ())),
                        preferred_element_type=jnp.float32,
                    )
                    for q in range(4):
                        for m in range(4):
                            across = slice(m * 128, (m + 1) * 128)
                            upper, lower = (
                                [
                                    product[e * 64 + q * 16 + h * 8 :, across][:8]
                                    for e in range(2)
                                ]
                                for h in range(2)
                            )
                            deliver(upper, lower, n * 4 + q, m)
            else:
                first_core = core == 0
                for n in range(4):
                    product = own_sum[n] + half_product(n, 1 - core)
                    for q in range(2):
                        for m in range(4):
                            across = slice(m * 128, (m + 1) * 128)
                            upper, lower = (
                                [
                                    jnp.where(
                                        first_core,
                                        product[q * 64 + h * 16 + e * 8 :, across][:8],
                                        product[q * 64 + 32 + h * 16 + e * 8 :, across][:8],
                                    )
                                    for e in range(2)
                                ]
                                for h in range(2)
                            )
                            deliver(upper, lower, n * 2 + q, m)
            send_products(u, g)

        for g in range(2):
            wait_bytes(prod_r.at[u], recv_sem.at[8 + u * 2 + g], CHIPS - 1)

            def unpack(q, carry):
                for col in range(8):
                    c = (q * 2 + g) * 8 + col
                    prod_f[pl.ds(pl.multiple_of(c * TILES, TILES), TILES), :] = prod_r[u, c].astype(
                        jnp.float32
                    )
                return carry

            lax.fori_loop(0, 8, unpack, 0)

        def finish(p, carry):
            product = jnp.concatenate(
                [prod_f[pl.ds(p * 2 + j, C, stride=TILES), :] for j in range(2)], axis=1
            )
            normout = normalise(product, wide(out_gain_t[u])).astype(jnp.bfloat16)
            update = jnp.dot(outw_t[u], normout, preferred_element_type=jnp.float32)
            new = (state[p] + gate[p] * update).astype(jnp.bfloat16).astype(jnp.float32)
            if u == 0:
                state[p] = new
            else:
                for j in range(2):
                    back = new[:, j * 128 : j * 128 + 128].T.astype(jnp.bfloat16)
                    out_ref[p * 2 + j] = back[0:COLS]
                    out_ref[p * 2 + j + HALF] = back[COLS : 2 * COLS]
            return carry

        def second(p, carry):
            project(1, p, state[p])
            return carry

        for part in range(PARTS):
            lax.fori_loop(part * 4, part * 4 + 4, finish, 0, unroll=4)
            if u == 0:
                lax.fori_loop(part * 4, part * 4 + 4, second, 0, unroll=4)
                pack(1, part, 0)
                send_sides(1, 0, part)
            else:
                for h in range(2):
                    stores[part * 2 + h].start()
        if u == 0:
            for part in range(PARTS):
                pack(1, part, 1)
            send_sides(1, 1, 0)

    for u in range(2):
        for g in range(2):
            if g == 0:
                for part in range(PARTS):
                    wait_bytes(prod_r.at[u], send_sem.at[u * 4 + part], CHIPS - 1)
            else:
                wait_bytes(sides_r.at[u, g], send_sem.at[u * 4 + 2], CHIPS - 1)
            wait_bytes(prod_s.at[u, g], send_sem.at[8 + u * 2 + g], CHIPS - 1)
    for g in range(2):
        wait_bytes(right_m.at[0, g], over_send.at[g], 256)
        for n in range(4):
            wait_bytes(right_m.at[1, g], over_send.at[2 + g * 4 + n], 128)
    for store in stores:
        store.wait()


def shards(pair, residue_mask, in_gain, proj_weight, gate_weight, out_gain, out_weight):
    return pl.pallas_call(
        kernel,
        out_shape=jax.ShapeDtypeStruct(pair.shape, pair.dtype),
        in_specs=[pl.BlockSpec(memory_space=pl.ANY)] * 7,
        out_specs=pl.BlockSpec(memory_space=pl.ANY),
        scratch_shapes=[
            pltpu.VMEM(pair.shape, pair.dtype),
            pltpu.SMEM(residue_mask.shape, residue_mask.dtype),
            pltpu.VMEM(pair.shape, pair.dtype),
            pltpu.VMEM(in_gain.shape, in_gain.dtype),
            pltpu.VMEM(proj_weight.shape, proj_weight.dtype),
            pltpu.VMEM(gate_weight.shape, gate_weight.dtype),
            pltpu.VMEM(out_gain.shape, out_gain.dtype),
            pltpu.VMEM(out_weight.shape, out_weight.dtype),
            pltpu.VMEM((2, 640, 128), jnp.bfloat16),
            pltpu.VMEM((2, 128, 128), jnp.bfloat16),
            pltpu.VMEM((2, 128, 128), jnp.float32),
            pltpu.VMEM((2, 128, 128), jnp.float32),
            pltpu.VMEM((PAIRS, 8, 256), jnp.float32),
            pltpu.VMEM((PAIRS, 128, 256), jnp.float32),
            pltpu.VMEM((PAIRS, 128, 256), jnp.float32),
            pltpu.VMEM((C * TILES, 128), jnp.float32),
            pltpu.VMEM((C * TILES, 128), jnp.float32),
            pltpu.VMEM((2, C, PARTS, 16, 128), jnp.bfloat16),
            pltpu.VMEM((2, 2, CHIPS, PARTS, 16, 128), jnp.bfloat16),
            pltpu.VMEM((2, 2, CHIPS, 16, 128), jnp.bfloat16),
            pltpu.VMEM((2, C, 16, 128), jnp.bfloat16),
            pltpu.VMEM((C * TILES, 128), jnp.float32),
            pltpu.VMEM((2, 256, 512), jnp.bfloat16),
            pltpu.VMEM((2, 512, 512), jnp.bfloat16),
            pltpu.VMEM((2, 2, 512, 512), jnp.bfloat16),
            pltpu.VMEM((4, 128, 512), jnp.float32),
            pltpu.SemaphoreType.DMA((7,)),
            pltpu.SemaphoreType.DMA((4,)),
            pltpu.SemaphoreType.DMA((10,)),
            pltpu.SemaphoreType.DMA((10,)),
            pltpu.SemaphoreType.DMA((12,)),
            pltpu.SemaphoreType.DMA((12,)),
        ],
        compiler_params=pltpu.CompilerParams(
            collective_id=0, has_side_effects=True, vmem_limit_bytes=58 * 1024 * 1024
        ),
    )(residue_mask, pair, in_gain, proj_weight, gate_weight, out_gain, out_weight)


def solution(mesh):
    placed = (P("row", "col", None), P(), P(), P(), P(), P(), P())
    return jax.shard_map(
        shards, mesh=mesh, in_specs=placed, out_specs=P("row", "col", None), check_vma=False
    )
```
